32 devices in a mesh: tm: 4 (over y, x), tile: 8 (over z, core).
Axes of the slice: x: 2, y: 2, z: 4, core: 2. Of those that a mesh axis runs over, the one named last changes fastest.
Arguments:
- frame_feats: bfloat16 [4, 64, 128, 1024], P(None, None, 'tile', 'tm'), may hold values from -6 to 6
- send_list: int32 [4, 4, 8, 3, 8], P(None, 'tm', 'tile'), may hold values from 0 to 15
- recv_slot: int32 [4, 4, 8, 16], P(None, 'tm', 'tile'), may hold values from 0 to 23, as said below
- w_unite: bfloat16 [3, 3, 64, 128], replicated, may hold values from -0.1875 to 0.1875
- w_inner: bfloat16 [3, 3, 64, 64], replicated, may hold values from -0.25 to 0.25
- w_outer: bfloat16 [3, 3, 64, 64], replicated, may hold values from -0.25 to 0.25
- w_up: bfloat16 [48, 64], replicated, may hold values from -0.75 to 0.75
Outputs:
- images: bfloat16 [4, 48, 128, 1024], P(None, None, 'tile', 'tm')
The draws below stay inside these ranges and needn't reach their ends.
Inputs may be any that keep to these rules, and one draw needn't show every extreme that they name: `send_list`: A block index within one band's part of a strip. recv_slot = o*8 + c names entry c of list o of band j + o - 1 in the same strip; band 0 never uses o = 0 and the last band never uses o = 2; for each frame, strip and band, the entries named from one list are 0 .. k-1 with k at most 8, each named once, and some list is named in all 8 entries.
All inputs are finite; a program needn't handle non-finite values.
Results may differ from the reference program's by a relative error of at most 0.019.
Values may be sent and summed in bfloat16 or wider, within the bound.
A program may use at most 64 MiB of HBM per device.

```python
import jax
import jax.numpy as jnp

C = 64
BLK = 16
NB = 16
FRAMES = 4
UP = 4
CAP = 8
HGT = 128
WID = 1024
N_TM = 4
N_TILE = 8


def draw_recv_slot(key, part):
    key_hot = jax.random.fold_in(key, 11)
    key_split = jax.random.fold_in(key, 12)
    key_rank = jax.random.fold_in(key, 13)
    grid = (FRAMES, N_TM, N_TILE)
    hot = jax.random.randint(key_hot, grid, 0, 3)
    split = jax.random.randint(key_split, grid, 0, CAP + 1)
    first = jnp.where(hot == 0, CAP, split)
    second = jnp.where(hot == 1, CAP, jnp.where(hot == 0, split, CAP - split))
    bands = jnp.arange(N_TILE, dtype=jnp.int32)[None, None, :]
    top_band = bands == 0
    low_band = bands == N_TILE - 1
    first = jnp.where(top_band, 0, jnp.where(low_band, CAP, first))
    second = jnp.where(top_band | low_band, CAP, second)
    keys = jax.random.split(key_rank, FRAMES * N_TM * N_TILE)
    ranks = jax.vmap(lambda single: jax.random.permutation(single, NB))(keys).reshape(FRAMES, N_TM, N_TILE, NB)
    first = first[..., None]
    second = second[..., None]
    slots = jnp.where(ranks < first, ranks, jnp.where(ranks < first + second, CAP + ranks - first, 2 * CAP + ranks - first - second))
    return slots.astype(jnp.int32)


def set_ends(entries, stream_key, low, top_value):
    extent = entries.shape
    place = [jax.random.randint(jax.random.fold_in(stream_key, axis), (), 0, extent[axis]) for axis in range(len(extent))]
    entries = entries.at[tuple(place)].set(low)
    longest = extent.index(max(extent))
    place[longest] = (place[longest] + 1) % extent[longest]
    return entries.at[tuple(place)].set(top_value)


def shard_levels(own_key, shape, shards, smallest, largest):
    gain = 1.0
    for dim, blocks in shards:
        draws = jax.random.uniform(jax.random.fold_in(jax.random.fold_in(own_key, 6), dim), (blocks,), jnp.float32, smallest / len(shards), largest / len(shards))
        gain = gain * jnp.repeat(jnp.exp(draws), shape[dim] // blocks).reshape((-1,) + (1,) * (len(shape) - 1 - dim))
    return gain


def centred(own_key, shape, spread, reach, shards=(), kind=jnp.bfloat16):
    loudness = shard_levels(own_key, shape, shards, -0.22, 0.18) if shards else 1.0
    result = jax.random.normal(own_key, shape, jnp.float32) * spread * loudness
    return jnp.minimum(jnp.maximum(result, -reach), reach).astype(kind)


def setup_inputs(seed: int = 0) -> dict:
    key_of = jax.random.split(jax.random.key(seed), 8)
    frame_feats = centred(key_of[0], (FRAMES, C, HGT, WID), 1.0, 6.0, ((2, 8), (3, 4)))
    send_list = set_ends(jax.random.randint(key_of[1], (FRAMES, N_TM, N_TILE, 3, CAP), 0, NB), jax.random.fold_in(key_of[1], 1), 0, NB - 1).astype(jnp.int32)
    recv_slot = draw_recv_slot(jax.random.fold_in(key_of[7], 71), 0)
    w_unite = centred(key_of[3], (3, 3, C, 2 * C), (18 * C) ** -0.5, 0.1875)
    w_inner = centred(key_of[4], (3, 3, C, C), (9 * C) ** -0.5, 0.25)
    w_outer = centred(key_of[5], (3, 3, C, C), (9 * C) ** -0.5, 0.25)
    w_up = centred(key_of[6], (3 * UP * UP, C), C ** -0.5, 0.75)
    return {"frame_feats": frame_feats, "send_list": send_list, "recv_slot": recv_slot, "w_unite": w_unite, "w_inner": w_inner, "w_outer": w_outer, "w_up": w_up}


def convolve(source, taps):
    in_chan, rows, cols = source.shape
    padded = jnp.pad(source, ((0, 0), (1, 1), (1, 1)))
    total = jnp.zeros((taps.shape[2], rows * cols), jnp.float32)
    for row_tap in range(3):
        for col_tap in range(3):
            window = padded[:, row_tap:row_tap + rows, col_tap:col_tap + cols].reshape(in_chan, rows * cols)
            total = total + jnp.dot(taps[row_tap, col_tap], window, preferred_element_type=jnp.float32)
    return total.reshape(taps.shape[2], rows, cols)


def warp_blocks(state, lists, slots):
    blocks = state.reshape(C, N_TILE, BLK, N_TM, NB, BLK)
    strips = jnp.arange(N_TM, dtype=jnp.int32)[:, None, None]
    bands = jnp.arange(N_TILE, dtype=jnp.int32)[None, :, None]
    offset = (slots // CAP).astype(jnp.int32)
    entry = (slots % CAP).astype(jnp.int32)
    source_band = jnp.clip(bands + offset - 1, 0, N_TILE - 1).astype(jnp.int32)
    strip_full = jnp.broadcast_to(strips, offset.shape).astype(jnp.int32)
    source_block = lists[strip_full, source_band, offset, entry].astype(jnp.int32)
    picked = blocks[:, source_band, :, strip_full, source_block, :]
    return picked.transpose(3, 1, 4, 0, 2, 5).reshape(C, HGT, WID)


def reference(frame_feats, send_list, recv_slot, w_unite, w_inner, w_outer, w_up):
    state = jnp.zeros((C, HGT, WID), jnp.bfloat16)
    images = []
    for frame in range(FRAMES):
        warped = warp_blocks(state, send_list[frame], recv_slot[frame])
        joined = jnp.concatenate([warped, frame_feats[frame]], 0)
        united = convolve(joined, w_unite).astype(jnp.bfloat16)
        inner = jax.nn.relu(convolve(united, w_inner)).astype(jnp.bfloat16)
        state = (united.astype(jnp.float32) + convolve(inner, w_outer)).astype(jnp.bfloat16)
        upper = jnp.dot(w_up, state.reshape(C, HGT * WID), preferred_element_type=jnp.float32)
        images.append(upper.reshape(3 * UP * UP, HGT, WID).astype(jnp.bfloat16))
    return jnp.stack(images, 0)
```

```python
import functools

import jax
import jax.numpy as jnp
from jax import lax
from jax.experimental import pallas as pl
from jax.experimental.pallas import tpu as pltpu
from jax.sharding import PartitionSpec as P

MESH = pl.DeviceIdType.MESH
HALO = 3
GROUPS = 4
SPAN = 32
LANES = GROUPS * SPAN
bf16 = jnp.bfloat16
f32 = jnp.float32


def taps_matrix(taps):
    kr, kc, out, inp = taps.shape
    return taps.transpose(1, 2, 0, 3).reshape(kc * out, kr * inp)


def conv_slab(weights, slab):
    part = jnp.dot(weights, slab, preferred_element_type=f32)
    out, n = part.shape[0] // 3, part.shape[1]
    left = pltpu.roll(part[0:out], 1, 1)
    right = pltpu.roll(part[2 * out : 3 * out], n - 1, 1)
    return left + part[out : 2 * out] + right


def looped(first, count, step, body):
    def go(i, carry):
        for k in range(step):
            body(first + i * step + k)
        return carry

    lax.fori_loop(0, count // step, go, 0)


def kernel(
    n_tm, n_tile, frames, chan, rows, cols,
    feats_ref, tgt_ref, src_ref, wu_ref, wi_ref, wo_ref, wp_ref,
    out_ref,
    join, united, inner, state, offer, pool, zone, zone_l, zone_r, edge, e_unit, e_inner, e_state, packer, patcher,
    load_sem, fr_send, fr_recv, wr_send, wr_recv, blk_send, blk_recv, zf_send, zf_recv, zw_send, zw_recv,
):
    strip = lax.axis_index("tm")
    band = lax.axis_index("tile")
    has_up, has_down = band > 0, band < n_tile - 1
    has_left, has_right = strip > 0, strip < n_tm - 1
    height, width = n_tile * rows, n_tm * cols
    full = rows + 2 * HALO
    qn = rows // GROUPS + 2 * HALO
    per = rows // GROUPS
    entries = tgt_ref.shape[2] // 3

    def load(f):
        return pltpu.make_async_copy(
            feats_ref.at[f], join.at[f, pl.ds(HALO, rows), pl.ds(chan, chan), :], load_sem.at[f]
        )

    for f in range(frames):
        load(f).start()

    up, down = {"tile": band - 1}, {"tile": band + 1}
    left, right = {"tm": strip - 1}, {"tm": strip + 1}
    sides = ((has_up, up), (has_down, down), (has_left, left), (has_right, right))

    join[:, 0:HALO] = jnp.zeros((frames, HALO, 2 * chan, cols), bf16)
    join[:, HALO + rows : full] = jnp.zeros((frames, HALO, 2 * chan, cols), bf16)
    join[0, HALO : HALO + rows, 0:chan] = jnp.zeros((rows, chan, cols), bf16)
    pool[...] = jnp.zeros(pool.shape, bf16)
    zone[0, :, 0:chan] = jnp.zeros((qn, chan, LANES), bf16)
    zone_l[...] = jnp.zeros(zone_l.shape, bf16)
    zone_r[...] = jnp.zeros(zone_r.shape, bf16)

    barrier = pltpu.get_barrier_semaphore()
    for there, device in sides:
        @pl.when(there)
        def _():
            pl.semaphore_signal(barrier, inc=1, device_id=device, device_id_type=MESH)

    lane = lax.broadcasted_iota(jnp.int32, (cols, LANES), 1)
    column = lax.broadcasted_iota(jnp.int32, (cols, LANES), 0)
    inside = lane % SPAN
    half = SPAN // 2
    wanted = jnp.where(
        inside < HALO,
        cols - HALO + inside,
        jnp.where(
            inside < half,
            inside - HALO,
            jnp.where(inside < SPAN - HALO, cols + HALO - SPAN + inside, inside - (SPAN - HALO)),
        ),
    )
    p_lane = lax.broadcasted_iota(jnp.int32, (LANES, cols), 0)
    p_col = lax.broadcasted_iota(jnp.int32, (LANES, cols), 1)
    p_in = p_lane % SPAN
    for g in range(GROUPS):
        packer[g] = ((lane // SPAN == g) & (column == wanted)).astype(f32).astype(bf16)
        here = jnp.where(p_in < half, p_in - HALO, cols + HALO - SPAN + p_in)
        near = (p_col < HALO) | (p_col >= cols - HALO)
        patcher[g] = ((p_lane // SPAN == g) & near & (here == p_col)).astype(f32).astype(bf16)

    pl.semaphore_wait(barrier, sum(there.astype(jnp.int32) for there, _ in sides))

    def remote(src, dst, send, recv, device):
        return pltpu.make_async_remote_copy(
            src_ref=src, dst_ref=dst, send_sem=send, recv_sem=recv, device_id=device, device_id_type=MESH
        )

    def row_pair(f, base, send, recv):
        part = pl.ds(base, chan)
        return (
            (has_up, remote(join.at[f, pl.ds(HALO, HALO), part, :], join.at[f, pl.ds(HALO + rows, HALO), part, :],
                            send.at[f, 0], recv.at[f, 0], up), has_down),
            (has_down, remote(join.at[f, pl.ds(rows, HALO), part, :], join.at[f, pl.ds(0, HALO), part, :],
                              send.at[f, 1], recv.at[f, 1], down), has_up),
        )

    def block_pair(f):
        low, high = pl.ds(0, entries), pl.ds(2 * entries, entries)
        return (
            (has_down, remote(offer.at[f, :, :, low], pool.at[f, :, :, low],
                              blk_send.at[f, 0], blk_recv.at[f, 0], down), has_up),
            (has_up, remote(offer.at[f, :, :, high], pool.at[f, :, :, high],
                            blk_send.at[f, 1], blk_recv.at[f, 1], up), has_down),
        )

    def zone_pair(f, base, send, recv):
        part = pl.ds(base, chan)
        return (
            (has_right, remote(zone.at[f, :, part, :], zone_l.at[f, :, part, :],
                               send.at[f, 0], recv.at[f, 0], right), has_left),
            (has_left, remote(zone.at[f, :, part, :], zone_r.at[f, :, part, :],
                              send.at[f, 1], recv.at[f, 1], left), has_right),
        )

    def start(pair):
        for sends, copy, _ in pair:
            pl.when(sends)(copy.start)

    def arrive(pair):
        for _, copy, gets in pair:
            pl.when(gets)(copy.wait_recv)

    def sent(pair):
        for sends, copy, _ in pair:
            pl.when(sends)(copy.wait_send)

    def pack_zone(f, base):
        total = jnp.zeros((qn * chan, LANES), f32)
        for g in range(GROUPS):
            part = join[f, per * g : per * g + qn, base : base + chan, :].reshape(qn * chan, cols)
            total = total + jnp.dot(part, packer[g], preferred_element_type=f32)
        zone[f, :, base : base + chan, :] = total.astype(bf16).reshape(qn, chan, LANES)

    for f in range(frames):
        load(f).wait()
        start(row_pair(f, chan, fr_send, fr_recv))

    e_lane = lax.broadcasted_iota(jnp.int32, (1, LANES), 1)
    e_in = e_lane % SPAN
    e_col = strip * cols + jnp.where(e_in < half, e_in - HALO, cols + HALO - SPAN + e_in)
    col_ok = (e_col >= 0) & (e_col < width)
    e_row = band * rows + per * (e_lane // SPAN) - HALO

    def edge_ok(q):
        row = e_row + q
        return col_ok & (row >= 0) & (row < height)

    def unite_row(f, r):
        return conv_slab(wu_ref[...], join[f, pl.ds(r - 1, 3)].reshape(6 * chan, cols))

    def frame(f, carry):
        arrive(row_pair(f, chan, fr_send, fr_recv))
        pack_zone(f, chan)
        start(zone_pair(f, chan, zf_send, zf_recv))

        @pl.when(f > 0)
        def _():
            arrive(block_pair(f))
            index = lax.broadcasted_iota(jnp.int32, (3 * entries, cols), 0)
            placer = (index == src_ref[f]).astype(f32).astype(bf16)
            warped = jnp.dot(pool[f].reshape(rows * chan, 3 * entries), placer, preferred_element_type=f32)
            join[f, HALO : HALO + rows, 0:chan, :] = warped.astype(bf16).reshape(rows, chan, cols)
            start(row_pair(f, 0, wr_send, wr_recv))

        def unite_inside(r):
            united[r] = unite_row(f, r).astype(bf16)

        looped(HALO + 1, rows - 2, 7, unite_inside)

        @pl.when(f > 0)
        def _():
            arrive(row_pair(f, 0, wr_send, wr_recv))
            pack_zone(f, 0)
            start(zone_pair(f, 0, zw_send, zw_recv))

        for r in (1, 2, HALO):
            value = unite_row(f, r)
            united[r] = (value if r == HALO else jnp.where(has_up, value, 0.0)).astype(bf16)
        for r in (HALO + rows - 1, HALO + rows, HALO + rows + 1):
            value = unite_row(f, r)
            united[r] = (value if r < HALO + rows else jnp.where(has_down, value, 0.0)).astype(bf16)

        def inner_row(r):
            slab = united[pl.ds(r - 1, 3)].reshape(3 * chan, cols)
            return jnp.maximum(conv_slab(wi_ref[...], slab), 0.0)

        def inner_inside(r):
            inner[r] = inner_row(r).astype(bf16)

        looped(HALO, rows, 4, inner_inside)
        inner[2] = jnp.where(has_up, inner_row(2), 0.0).astype(bf16)
        inner[HALO + rows] = jnp.where(has_down, inner_row(HALO + rows), 0.0).astype(bf16)

        def outer_row(r):
            slab = inner[pl.ds(r - 1, 3)].reshape(3 * chan, cols)
            state[r - HALO] = (united[r].astype(f32) + conv_slab(wo_ref[...], slab)).astype(bf16)

        looped(HALO, rows, 4, outer_row)

        arrive(zone_pair(f, chan, zf_send, zf_recv))

        @pl.when(f > 0)
        def _():
            arrive(zone_pair(f, 0, zw_send, zw_recv))

        for q in range(qn):
            own, before, after = zone[f, q], zone_l[f, q], zone_r[f, q]
            edge[q] = jnp.where(e_in < HALO, before, jnp.where(e_in >= SPAN - HALO, after, own))
        for q in range(1, qn - 1):
            value = conv_slab(wu_ref[...], edge[q - 1 : q + 2].reshape(6 * chan, LANES))
            e_unit[q] = jnp.where(edge_ok(q), value, 0.0).astype(bf16)
        for q in range(2, qn - 2):
            value = conv_slab(wi_ref[...], e_unit[q - 1 : q + 2].reshape(3 * chan, LANES))
            e_inner[q] = jnp.where(edge_ok(q), jnp.maximum(value, 0.0), 0.0).astype(bf16)
        for q in range(3, qn - 3):
            value = conv_slab(wo_ref[...], e_inner[q - 1 : q + 2].reshape(3 * chan, LANES))
            e_state[q - 3] = (e_unit[q].astype(f32) + value).astype(bf16)

        ends = e_state[...].reshape(per * chan, LANES)
        spot = lax.broadcasted_iota(jnp.int32, (per * chan, cols), 1)
        near = (spot < HALO) | (spot >= cols - HALO)
        for g in range(GROUPS):
            patch = jnp.dot(ends, patcher[g], preferred_element_type=f32)
            old = state[per * g : per * (g + 1)].reshape(per * chan, cols).astype(f32)
            state[per * g : per * (g + 1)] = jnp.where(near, patch, old).astype(bf16).reshape(per, chan, cols)

        @pl.when(f < frames - 1)
        def _():
            index = lax.broadcasted_iota(jnp.int32, (cols, 3 * entries), 0)
            picker = (index == tgt_ref[f + 1]).astype(f32).astype(bf16)
            picked = jnp.dot(state[...].reshape(rows * chan, cols), picker, preferred_element_type=f32)
            picked = picked.astype(bf16).reshape(rows, chan, 3 * entries)
            offer[f + 1] = picked
            pool[f + 1, :, :, entries : 2 * entries] = picked[:, :, entries : 2 * entries]
            start(block_pair(f + 1))

        for r in range(rows):
            out_ref[f, r] = jnp.dot(wp_ref[...], state[r], preferred_element_type=f32).astype(bf16)

        sent(row_pair(f, chan, fr_send, fr_recv))
        sent(zone_pair(f, chan, zf_send, zf_recv))

        @pl.when(f > 0)
        def _():
            sent(row_pair(f, 0, wr_send, wr_recv))
            sent(zone_pair(f, 0, zw_send, zw_recv))
            sent(block_pair(f))

        return carry

    lax.fori_loop(0, frames, frame, 0)


def on_device(n_tm, n_tile, frame_feats, send_list, recv_slot, w_unite, w_inner, w_outer, w_up):
    frames, chan, rows, cols = frame_feats.shape
    planes = w_up.shape[0]
    feats = frame_feats.transpose(0, 2, 1, 3)
    inside = jnp.arange(rows, dtype=jnp.int32)
    lists = send_list[:, 0, 0].reshape(frames, -1)
    tgt = (lists[:, :, None] * rows + inside).reshape(frames, 1, -1)
    src = (recv_slot[:, 0, 0][:, :, None] * rows + inside).reshape(frames, 1, -1)
    width3 = tgt.shape[2]
    full = rows + 2 * HALO
    per = rows // GROUPS
    qn = per + 2 * HALO
    vmem = pl.BlockSpec(memory_space=pltpu.VMEM)
    sems = pltpu.SemaphoreType.DMA((frames, 2))
    out = pl.pallas_call(
        functools.partial(kernel, n_tm, n_tile, frames, chan, rows, cols),
        out_shape=jax.ShapeDtypeStruct((frames, rows, planes, cols), bf16),
        in_specs=[pl.BlockSpec(memory_space=pl.ANY)] + [vmem] * 6,
        out_specs=vmem,
        scratch_shapes=[
            pltpu.VMEM((frames, full, 2 * chan, cols), bf16),
            pltpu.VMEM((full, chan, cols), bf16),
            pltpu.VMEM((full, chan, cols), bf16),
            pltpu.VMEM((rows, chan, cols), bf16),
            pltpu.VMEM((frames, rows, chan, width3), bf16),
            pltpu.VMEM((frames, rows, chan, width3), bf16),
            pltpu.VMEM((frames, qn, 2 * chan, LANES), bf16),
            pltpu.VMEM((frames, qn, 2 * chan, LANES), bf16),
            pltpu.VMEM((frames, qn, 2 * chan, LANES), bf16),
            pltpu.VMEM((qn, 2 * chan, LANES), bf16),
            pltpu.VMEM((qn, chan, LANES), bf16),
            pltpu.VMEM((qn, chan, LANES), bf16),
            pltpu.VMEM((per, chan, LANES), bf16),
            pltpu.VMEM((GROUPS, cols, LANES), bf16),
            pltpu.VMEM((GROUPS, LANES, cols), bf16),
            pltpu.SemaphoreType.DMA((frames,)),
        ] + [sems] * 10,
        compiler_params=pltpu.CompilerParams(
            collective_id=0, has_side_effects=True, vmem_limit_bytes=48 * 1024 * 1024
        ),
        name="propagate",
    )(feats, tgt, src, taps_matrix(w_unite), taps_matrix(w_inner), taps_matrix(w_outer), w_up)
    return out.transpose(0, 2, 1, 3)


def solution(mesh):
    placed = (
        P(None, None, "tile", "tm"),
        P(None, "tm", "tile", None, None),
        P(None, "tm", "tile", None),
        P(),
        P(),
        P(),
        P(),
    )
    return jax.shard_map(
        functools.partial(on_device, mesh.shape["tm"], mesh.shape["tile"]),
        mesh=mesh,
        in_specs=placed,
        out_specs=P(None, None, "tile", "tm"),
        check_vma=False,
    )
```

```python
import functools

import jax
import jax.numpy as jnp
from jax import lax
from jax.experimental import pallas as pl
from jax.experimental.pallas import tpu as pltpu
from jax.sharding import PartitionSpec as P

MESH = pl.DeviceIdType.MESH
HALO = 3
GROUPS = 4
SPAN = 32
LANES = GROUPS * SPAN
bf16 = jnp.bfloat16
f32 = jnp.float32


def lay_taps(taps_ref, matrix):
    kr, kc, out, inp = taps_ref.shape
    for b in range(kc):
        parts = [taps_ref[a, b].astype(f32) for a in range(kr)]
        matrix[b * out : (b + 1) * out] = jnp.concatenate(parts, 1).astype(bf16)


def conv_slab(weights, slab):
    part = jnp.dot(weights, slab, preferred_element_type=f32)
    out, n = part.shape[0] // 3, part.shape[1]
    left = pltpu.roll(part[0:out], 1, 1)
    right = pltpu.roll(part[2 * out : 3 * out], n - 1, 1)
    return left + part[out : 2 * out] + right


def kernel(
    n_tm, n_tile, frames, chan, rows, cols,
    feats_ref, list_ref, slot_ref, tu_ref, ti_ref, to_ref, wp_ref,
    out_ref,
    wu_ref, wi_ref, wo_ref, join, united, inner, state, offer, pool, zone, zone_s, zone_l, zone_r, edge, e_unit, e_inner, e_state, packer, patcher,
    load_sem, fr_send, fr_recv, wr_send, wr_recv, blk_send, blk_recv, zf_send, zf_recv, zw_send, zw_recv,
):
    strip = lax.axis_index("tm")
    band = lax.axis_index("tile")
    has_up, has_down = band > 0, band < n_tile - 1
    has_left, has_right = strip > 0, strip < n_tm - 1
    height, width = n_tile * rows, n_tm * cols
    full = rows + 2 * HALO
    qn = rows // GROUPS + 2 * HALO
    per = rows // GROUPS
    cap = list_ref.shape[4]
    blocks = slot_ref.shape[3]
    entries = cap * rows

    def load(f):
        return pltpu.make_async_copy(
            feats_ref.at[f], join.at[f, pl.ds(HALO, rows), pl.ds(chan, chan), :], load_sem.at[f]
        )

    for f in range(frames):
        load(f).start()

    up, down = {"tile": band - 1}, {"tile": band + 1}
    left, right = {"tm": strip - 1}, {"tm": strip + 1}
    sides = ((has_up, up), (has_down, down), (has_left, left), (has_right, right))

    join[0, :, 0:chan] = jnp.zeros((full, chan, cols), bf16)
    zone[0, :, 0:chan] = jnp.zeros((qn, chan, LANES), bf16)
    zone_l[0, 0:chan] = jnp.zeros((chan, LANES), bf16)
    zone_r[0, 0:chan] = jnp.zeros((chan, LANES), bf16)

    @pl.when(jnp.logical_not(has_up))
    def _():
        join[:, 0:HALO] = jnp.zeros((frames, HALO, 2 * chan, cols), bf16)
        pool[:, 0] = jnp.zeros((frames, rows, chan, entries), bf16)

    @pl.when(jnp.logical_not(has_down))
    def _():
        join[:, HALO + rows : full] = jnp.zeros((frames, HALO, 2 * chan, cols), bf16)
        pool[:, 2] = jnp.zeros((frames, rows, chan, entries), bf16)

    @pl.when(jnp.logical_not(has_left))
    def _():
        zone_l[...] = jnp.zeros(zone_l.shape, bf16)

    @pl.when(jnp.logical_not(has_right))
    def _():
        zone_r[...] = jnp.zeros(zone_r.shape, bf16)

    barrier = pltpu.get_barrier_semaphore()
    for there, device in sides:
        @pl.when(there)
        def _():
            pl.semaphore_signal(barrier, inc=1, device_id=device, device_id_type=MESH)

    lane = lax.broadcasted_iota(jnp.int32, (cols, LANES), 1)
    column = lax.broadcasted_iota(jnp.int32, (cols, LANES), 0)
    inside = lane % SPAN
    half = SPAN // 2
    wanted = jnp.where(
        inside < HALO,
        cols - HALO + inside,
        jnp.where(
            inside < half,
            inside - HALO,
            jnp.where(inside < SPAN - HALO, cols + HALO - SPAN + inside, inside - (SPAN - HALO)),
        ),
    )
    p_lane = lax.broadcasted_iota(jnp.int32, (LANES, cols), 0)
    p_col = lax.broadcasted_iota(jnp.int32, (LANES, cols), 1)
    p_in = p_lane % SPAN
    for g in range(GROUPS):
        packer[g] = ((lane // SPAN == g) & (column == wanted)).astype(f32).astype(bf16)
        here = jnp.where(p_in < half, p_in - HALO, cols + HALO - SPAN + p_in)
        near = (p_col < HALO) | (p_col >= cols - HALO)
        patcher[g] = ((p_lane // SPAN == g) & near & (here == p_col)).astype(f32).astype(bf16)

    pl.semaphore_wait(barrier, sum(there.astype(jnp.int32) for there, _ in sides))

    def remote(src, dst, send, recv, device):
        return pltpu.make_async_remote_copy(
            src_ref=src, dst_ref=dst, send_sem=send, recv_sem=recv, device_id=device, device_id_type=MESH
        )

    def row_pair(f, base, send, recv):
        part = pl.ds(base, chan)
        return (
            (has_up, remote(join.at[f, pl.ds(HALO, HALO), part, :], join.at[f, pl.ds(HALO + rows, HALO), part, :],
                            send.at[f, 0], recv.at[f, 0], up), has_down),
            (has_down, remote(join.at[f, pl.ds(rows, HALO), part, :], join.at[f, pl.ds(0, HALO), part, :],
                              send.at[f, 1], recv.at[f, 1], down), has_up),
        )

    def block_pair(f):
        return (
            (has_down, remote(offer.at[f, 0], pool.at[f, 0],
                              blk_send.at[f, 0], blk_recv.at[f, 0], down), has_up),
            (has_up, remote(offer.at[f, 1], pool.at[f, 2],
                            blk_send.at[f, 1], blk_recv.at[f, 1], up), has_down),
        )

    def zone_pair(f, base, send, recv):
        part = pl.ds(base, chan)
        return (
            (has_right, remote(zone_s.at[f, 0, part, :], zone_l.at[f, part, :],
                               send.at[f, 0], recv.at[f, 0], right), has_left),
            (has_left, remote(zone_s.at[f, 1, part, :], zone_r.at[f, part, :],
                              send.at[f, 1], recv.at[f, 1], left), has_right),
        )

    def start(pair):
        for sends, copy, _ in pair:
            pl.when(sends)(copy.start)

    def arrive(pair):
        for _, copy, gets in pair:
            pl.when(gets)(copy.wait_recv)

    def sent(pair):
        for sends, copy, _ in pair:
            pl.when(sends)(copy.wait_send)

    e_lane = lax.broadcasted_iota(jnp.int32, (1, LANES), 1)
    e_in = e_lane % SPAN

    def pack_zone(f, base):
        total = jnp.zeros((qn * chan, LANES), f32)
        for g in range(GROUPS):
            part = join[f, per * g : per * g + qn, base : base + chan, :].reshape(qn * chan, cols)
            total = total + jnp.dot(part, packer[g], preferred_element_type=f32)
        total = total.reshape(qn, chan, LANES)
        zone[f, :, base : base + chan, :] = total.astype(bf16)
        last, first = total[0], pltpu.roll(total[0], LANES - (SPAN - HALO), 1)
        for q in range(1, qn):
            here = (e_in >= HALO * q) & (e_in < HALO * (q + 1))
            last = jnp.where(here, pltpu.roll(total[q], HALO * q, 1), last)
            first = jnp.where(here, pltpu.roll(total[q], (LANES - (SPAN - HALO) + HALO * q) % LANES, 1), first)
        zone_s[f, 0, base : base + chan, :] = last.astype(bf16)
        zone_s[f, 1, base : base + chan, :] = first.astype(bf16)

    for f in range(frames):
        load(f).wait()
        start(row_pair(f, chan, fr_send, fr_recv))

    lay_taps(tu_ref, wu_ref)
    lay_taps(ti_ref, wi_ref)
    lay_taps(to_ref, wo_ref)

    e_col = strip * cols + jnp.where(e_in < half, e_in - HALO, cols + HALO - SPAN + e_in)
    col_ok = (e_col >= 0) & (e_col < width)
    e_row = band * rows + per * (e_lane // SPAN) - HALO

    def edge_ok(q):
        row = e_row + q
        return col_ok & (row >= 0) & (row < height)

    def unite_row(f, r):
        return conv_slab(wu_ref[...], join[f, pl.ds(r - 1, 3)].reshape(6 * chan, cols))

    def frame(f, carry):
        arrive(row_pair(f, chan, fr_send, fr_recv))
        pack_zone(f, chan)
        start(zone_pair(f, chan, zf_send, zf_recv))

        @pl.when(f > 0)
        def _():
            arrive(block_pair(f))
            spot = lax.broadcasted_iota(jnp.int32, (1, cols), 1)
            source = jnp.zeros((1, cols), jnp.int32)
            for d in range(blocks):
                source = jnp.where(spot // rows == d, slot_ref[f, 0, 0, d] * rows, source)
            index = lax.broadcasted_iota(jnp.int32, (3 * entries, cols), 0)
            placer = (index == source + spot % rows).astype(f32).astype(bf16)
            whole = jnp.concatenate([pool[f, o].reshape(rows * chan, entries) for o in range(3)], 1)
            warped = jnp.dot(whole, placer, preferred_element_type=f32)
            join[f, HALO : HALO + rows, 0:chan, :] = warped.astype(bf16).reshape(rows, chan, cols)
            start(row_pair(f, 0, wr_send, wr_recv))

        for r in range(HALO + 1, HALO + rows - 1):
            united[r] = unite_row(f, r).astype(bf16)

        @pl.when(f > 0)
        def _():
            arrive(row_pair(f, 0, wr_send, wr_recv))
            pack_zone(f, 0)
            start(zone_pair(f, 0, zw_send, zw_recv))

        for r in (1, 2, HALO):
            value = unite_row(f, r)
            united[r] = (value if r == HALO else jnp.where(has_up, value, 0.0)).astype(bf16)
        for r in (HALO + rows - 1, HALO + rows, HALO + rows + 1):
            value = unite_row(f, r)
            united[r] = (value if r < HALO + rows else jnp.where(has_down, value, 0.0)).astype(bf16)

        def inner_row(r):
            slab = united[pl.ds(r - 1, 3)].reshape(3 * chan, cols)
            return jnp.maximum(conv_slab(wi_ref[...], slab), 0.0)

        for r in range(HALO, HALO + rows):
            inner[r] = inner_row(r).astype(bf16)
        inner[2] = jnp.where(has_up, inner_row(2), 0.0).astype(bf16)
        inner[HALO + rows] = jnp.where(has_down, inner_row(HALO + rows), 0.0).astype(bf16)

        def outer_row(r):
            slab = inner[pl.ds(r - 1, 3)].reshape(3 * chan, cols)
            state[r - HALO] = (united[r].astype(f32) + conv_slab(wo_ref[...], slab)).astype(bf16)

        for r in range(HALO, HALO + rows):
            outer_row(r)

        arrive(zone_pair(f, chan, zf_send, zf_recv))

        @pl.when(f > 0)
        def _():
            arrive(zone_pair(f, 0, zw_send, zw_recv))

        from_l, from_r = zone_l[f].astype(f32), zone_r[f].astype(f32)
        for q in range(qn):
            before = pltpu.roll(from_l, (LANES - HALO * q) % LANES, 1)
            after = pltpu.roll(from_r, (LANES + SPAN - HALO - HALO * q) % LANES, 1)
            value = jnp.where(e_in < HALO, before, jnp.where(e_in >= SPAN - HALO, after, zone[f, q].astype(f32)))
            edge[q] = value.astype(bf16)
        for q in range(1, qn - 1):
            value = conv_slab(wu_ref[...], edge[q - 1 : q + 2].reshape(6 * chan, LANES))
            e_unit[q] = jnp.where(edge_ok(q), value, 0.0).astype(bf16)
        for q in range(2, qn - 2):
            value = conv_slab(wi_ref[...], e_unit[q - 1 : q + 2].reshape(3 * chan, LANES))
            e_inner[q] = jnp.where(edge_ok(q), jnp.maximum(value, 0.0), 0.0).astype(bf16)
        for q in range(3, qn - 3):
            value = conv_slab(wo_ref[...], e_inner[q - 1 : q + 2].reshape(3 * chan, LANES))
            e_state[q - 3] = (e_unit[q].astype(f32) + value).astype(bf16)

        ends = e_state[...].reshape(per * chan, LANES)
        spot = lax.broadcasted_iota(jnp.int32, (per * chan, cols), 1)
        near = (spot < HALO) | (spot >= cols - HALO)
        for g in range(GROUPS):
            patch = jnp.dot(ends, patcher[g], preferred_element_type=f32)
            old = state[per * g : per * (g + 1)].reshape(per * chan, cols).astype(f32)
            state[per * g : per * (g + 1)] = jnp.where(near, patch, old).astype(bf16).reshape(per, chan, cols)

        @pl.when(f < frames - 1)
        def _():
            spot = lax.broadcasted_iota(jnp.int32, (1, entries), 1)
            index = lax.broadcasted_iota(jnp.int32, (cols, entries), 0)
            whole = state[...].reshape(rows * chan, cols)
            pickers = []
            for o in (0, 2, 1):
                target = jnp.zeros((1, entries), jnp.int32)
                for c in range(cap):
                    target = jnp.where(spot // rows == c, list_ref[f + 1, 0, 0, o, c] * rows, target)
                pickers.append((index == target + spot % rows).astype(f32).astype(bf16))
            away = jnp.dot(whole, jnp.concatenate(pickers[:2], 1), preferred_element_type=f32).astype(bf16)
            offer[f + 1, 0] = away[:, :entries].reshape(rows, chan, entries)
            offer[f + 1, 1] = away[:, entries:].reshape(rows, chan, entries)
            start(block_pair(f + 1))
            kept = jnp.dot(whole, pickers[2], preferred_element_type=f32).astype(bf16)
            pool[f + 1, 1] = kept.reshape(rows, chan, entries)

        for r in range(rows):
            out_ref[f, r] = jnp.dot(wp_ref[...], state[r], preferred_element_type=f32).astype(bf16)

        sent(row_pair(f, chan, fr_send, fr_recv))
        sent(zone_pair(f, chan, zf_send, zf_recv))

        @pl.when(f > 0)
        def _():
            sent(row_pair(f, 0, wr_send, wr_recv))
            sent(zone_pair(f, 0, zw_send, zw_recv))
            sent(block_pair(f))

        return carry

    lax.fori_loop(0, frames, frame, 0)


def on_device(n_tm, n_tile, frame_feats, send_list, recv_slot, w_unite, w_inner, w_outer, w_up):
    frames, chan, rows, cols = frame_feats.shape
    planes = w_up.shape[0]
    feats = frame_feats.transpose(0, 2, 1, 3)
    entries = send_list.shape[4] * rows
    full = rows + 2 * HALO
    per = rows // GROUPS
    qn = per + 2 * HALO
    vmem = pl.BlockSpec(memory_space=pltpu.VMEM)
    smem = pl.BlockSpec(memory_space=pltpu.SMEM)
    sems = pltpu.SemaphoreType.DMA((frames, 2))
    out = pl.pallas_call(
        functools.partial(kernel, n_tm, n_tile, frames, chan, rows, cols),
        out_shape=jax.ShapeDtypeStruct((frames, rows, planes, cols), bf16),
        in_specs=[pl.BlockSpec(memory_space=pl.ANY)] + [smem] * 2 + [vmem] * 4,
        out_specs=vmem,
        scratch_shapes=[
            pltpu.VMEM((3 * chan, 6 * chan), bf16),
            pltpu.VMEM((3 * chan, 3 * chan), bf16),
            pltpu.VMEM((3 * chan, 3 * chan), bf16),
            pltpu.VMEM((frames, full, 2 * chan, cols), bf16),
            pltpu.VMEM((full, chan, cols), bf16),
            pltpu.VMEM((full, chan, cols), bf16),
            pltpu.VMEM((rows, chan, cols), bf16),
            pltpu.VMEM((frames, 2, rows, chan, entries), bf16),
            pltpu.VMEM((frames, 3, rows, chan, entries), bf16),
            pltpu.VMEM((frames, qn, 2 * chan, LANES), bf16),
            pltpu.VMEM((frames, 2, 2 * chan, LANES), bf16),
            pltpu.VMEM((frames, 2 * chan, LANES), bf16),
            pltpu.VMEM((frames, 2 * chan, LANES), bf16),
            pltpu.VMEM((qn, 2 * chan, LANES), bf16),
            pltpu.VMEM((qn, chan, LANES), bf16),
            pltpu.VMEM((qn, chan, LANES), bf16),
            pltpu.VMEM((per, chan, LANES), bf16),
            pltpu.VMEM((GROUPS, cols, LANES), bf16),
            pltpu.VMEM((GROUPS, LANES, cols), bf16),
            pltpu.SemaphoreType.DMA((frames,)),
        ] + [sems] * 10,
        compiler_params=pltpu.CompilerParams(
            collective_id=0, has_side_effects=True, vmem_limit_bytes=48 * 1024 * 1024
        ),
        name="propagate",
    )(feats, send_list, recv_slot, w_unite, w_inner, w_outer, w_up)
    return out.transpose(0, 2, 1, 3)


def solution(mesh):
    placed = (
        P(None, None, "tile", "tm"),
        P(None, "tm", "tile", None, None),
        P(None, "tm", "tile", None),
        P(),
        P(),
        P(),
        P(),
    )
    return jax.shard_map(
        functools.partial(on_device, mesh.shape["tm"], mesh.shape["tile"]),
        mesh=mesh,
        in_specs=placed,
        out_specs=P(None, None, "tile", "tm"),
        check_vma=False,
    )
```

```python
import functools

import jax
import jax.numpy as jnp
from jax import lax
from jax.experimental import pallas as pl
from jax.experimental.pallas import tpu as pltpu
from jax.sharding import PartitionSpec as P

MESH = pl.DeviceIdType.MESH
HALO = 3
GROUPS = 4
SPAN = 32
LANES = GROUPS * SPAN
PIECES = 2
bf16 = jnp.bfloat16
f32 = jnp.float32


def lay_taps(taps_ref, base, matrix):
    kr, kc, out, _ = taps_ref.shape
    inp = matrix.shape[1] // (kr + 1)
    blank = jnp.zeros((out, inp), f32)
    for p in range(2):
        for b in range(kc):
            parts = []
            for a in range(kr + 1):
                tap = a - p
                parts.append(taps_ref[tap, b][:, base : base + inp].astype(f32) if 0 <= tap < kr else blank)
            row = (p * kc + b) * out
            matrix[row : row + out] = jnp.concatenate(parts, 1).astype(bf16)


def conv_pair(weights, slab):
    part = jnp.dot(weights, slab, preferred_element_type=f32)
    out, n = part.shape[0] // 6, part.shape[1]
    rows = []
    for p in range(2):
        base = 3 * out * p
        left = pltpu.roll(part[base : base + out], 1, 1)
        right = pltpu.roll(part[base + 2 * out : base + 3 * out], n - 1, 1)
        rows.append(left + part[base + out : base + 2 * out] + right)
    return rows


def kernel(
    n_tm, n_tile, frames, chan, rows, cols,
    feats_ref, list_ref, slot_ref, tu_ref, ti_ref, to_ref, wp_ref,
    out_ref,
    ww_ref, wf_ref, wi_ref, wo_ref, feats, warped, partial, united, inner, state, offer, pool,
    zone_s, zone_r, zone_f, zone_w, edge, e_part, e_unit, e_inner, e_state, packer, patcher,
    load_sem, row_send, row_recv, blk_send, blk_recv, zone_send, zone_recv,
):
    strip = lax.axis_index("tm")
    band = lax.axis_index("tile")
    has_up, has_down = band > 0, band < n_tile - 1
    has_left, has_right = strip > 0, strip < n_tm - 1
    height, width = n_tile * rows, n_tm * cols
    full = rows + 2 * HALO
    per = rows // GROUPS
    qn = per + 2 * HALO
    cap = list_ref.shape[4]
    blocks = slot_ref.shape[3]
    entries = cap * rows
    piece = rows // PIECES

    def load(f):
        return pltpu.make_async_copy(feats_ref.at[f], feats.at[f, pl.ds(HALO, rows)], load_sem.at[f])

    for f in range(frames):
        load(f).start()

    up, down = {"tile": band - 1}, {"tile": band + 1}
    left, right = {"tm": strip - 1}, {"tm": strip + 1}
    sides = ((has_up, up), (has_down, down), (has_left, left), (has_right, right))

    @pl.when(jnp.logical_not(has_up))
    def _():
        feats[:, 0:HALO] = jnp.zeros((frames, HALO, chan, cols), bf16)
        warped[:, 0:HALO] = jnp.zeros((frames, HALO, chan, cols), bf16)
        pool[:, 0] = jnp.zeros((frames, rows, chan, entries), bf16)

    @pl.when(jnp.logical_not(has_down))
    def _():
        feats[:, HALO + rows : full] = jnp.zeros((frames, HALO, chan, cols), bf16)
        warped[:, HALO + rows : full] = jnp.zeros((frames, HALO, chan, cols), bf16)
        pool[:, 2] = jnp.zeros((frames, rows, chan, entries), bf16)

    @pl.when(jnp.logical_not(has_left))
    def _():
        zone_r[:, :, 0] = jnp.zeros((frames, 2, chan, LANES), bf16)

    @pl.when(jnp.logical_not(has_right))
    def _():
        zone_r[:, :, 1] = jnp.zeros((frames, 2, chan, LANES), bf16)

    barrier = pltpu.get_barrier_semaphore()
    for there, device in sides:
        @pl.when(there)
        def _():
            pl.semaphore_signal(barrier, inc=1, device_id=device, device_id_type=MESH)

    lane = lax.broadcasted_iota(jnp.int32, (cols, LANES), 1)
    column = lax.broadcasted_iota(jnp.int32, (cols, LANES), 0)
    inside = lane % SPAN
    half = SPAN // 2
    wanted = jnp.where(
        inside < HALO,
        cols - HALO + inside,
        jnp.where(
            inside < half,
            inside - HALO,
            jnp.where(inside < SPAN - HALO, cols + HALO - SPAN + inside, inside - (SPAN - HALO)),
        ),
    )
    p_lane = lax.broadcasted_iota(jnp.int32, (LANES, cols), 0)
    p_col = lax.broadcasted_iota(jnp.int32, (LANES, cols), 1)
    p_in = p_lane % SPAN
    for g in range(GROUPS):
        packer[g] = ((lane // SPAN == g) & (column == wanted)).astype(f32).astype(bf16)
        here = jnp.where(p_in < half, p_in - HALO, cols + HALO - SPAN + p_in)
        near = (p_col < HALO) | (p_col >= cols - HALO)
        patcher[g] = ((p_lane // SPAN == g) & near & (here == p_col)).astype(f32).astype(bf16)

    for f in range(frames):
        load(f).wait()

    pl.semaphore_wait(barrier, sum(there.astype(jnp.int32) for there, _ in sides))

    def remote(src, dst, send, recv, device):
        return pltpu.make_async_remote_copy(
            src_ref=src, dst_ref=dst, send_sem=send, recv_sem=recv, device_id=device, device_id_type=MESH
        )

    def row_pair(f, kind, ref):
        return (
            (has_up, remote(ref.at[f, pl.ds(HALO, HALO)], ref.at[f, pl.ds(HALO + rows, HALO)],
                            row_send.at[f, kind, 0], row_recv.at[f, kind, 0], up), has_down),
            (has_down, remote(ref.at[f, pl.ds(rows, HALO)], ref.at[f, pl.ds(0, HALO)],
                              row_send.at[f, kind, 1], row_recv.at[f, kind, 1], down), has_up),
        )

    def block_pair(f, h):
        part = pl.ds(piece * h, piece)
        return (
            (has_down, remote(offer.at[f, 0, part], pool.at[f, 0, part],
                              blk_send.at[f, h, 0], blk_recv.at[f, h, 0], down), has_up),
            (has_up, remote(offer.at[f, 1, part], pool.at[f, 2, part],
                            blk_send.at[f, h, 1], blk_recv.at[f, h, 1], up), has_down),
        )

    def zone_pair(f, kind):
        return (
            (has_right, remote(zone_s.at[f, kind, 0], zone_r.at[f, kind, 0],
                               zone_send.at[f, kind, 0], zone_recv.at[f, kind, 0], right), has_left),
            (has_left, remote(zone_s.at[f, kind, 1], zone_r.at[f, kind, 1],
                              zone_send.at[f, kind, 1], zone_recv.at[f, kind, 1], left), has_right),
        )

    def start(pair):
        for sends, copy, _ in pair:
            pl.when(sends)(copy.start)

    def arrive(pair):
        for _, copy, gets in pair:
            pl.when(gets)(copy.wait_recv)

    def sent(pair):
        for sends, copy, _ in pair:
            pl.when(sends)(copy.wait_send)

    for f in range(frames):
        start(row_pair(f, 0, feats))
    lay_taps(tu_ref, 0, ww_ref)
    lay_taps(tu_ref, chan, wf_ref)
    lay_taps(ti_ref, 0, wi_ref)
    lay_taps(to_ref, 0, wo_ref)

    e_lane = lax.broadcasted_iota(jnp.int32, (1, LANES), 1)
    e_in = e_lane % SPAN
    e_col = strip * cols + jnp.where(e_in < half, e_in - HALO, cols + HALO - SPAN + e_in)
    col_ok = (e_col >= 0) & (e_col < width)
    e_row = band * rows + per * (e_lane // SPAN) - HALO

    def edge_ok(q):
        row = e_row + q
        return col_ok & (row >= 0) & (row < height)

    def pack_zone(f, kind, ref, zone):
        total = jnp.zeros((qn * chan, LANES), f32)
        for g in range(GROUPS):
            part = ref[f, per * g : per * g + qn].reshape(qn * chan, cols)
            total = total + jnp.dot(part, packer[g], preferred_element_type=f32)
        total = total.reshape(qn, chan, LANES)
        zone[...] = total.astype(bf16)
        last, first = total[0], pltpu.roll(total[0], LANES - (SPAN - HALO), 1)
        for q in range(1, qn):
            here = (e_in >= HALO * q) & (e_in < HALO * (q + 1))
            last = jnp.where(here, pltpu.roll(total[q], HALO * q, 1), last)
            first = jnp.where(here, pltpu.roll(total[q], (LANES - (SPAN - HALO) + HALO * q) % LANES, 1), first)
        zone_s[f, kind, 0] = last.astype(bf16)
        zone_s[f, kind, 1] = first.astype(bf16)
        start(zone_pair(f, kind))

    def lay_edge(f, kind, zone):
        arrive(zone_pair(f, kind))
        from_l, from_r = zone_r[f, kind, 0].astype(f32), zone_r[f, kind, 1].astype(f32)
        for q in range(qn):
            before = pltpu.roll(from_l, (LANES - HALO * q) % LANES, 1)
            after = pltpu.roll(from_r, (LANES + SPAN - HALO - HALO * q) % LANES, 1)
            value = jnp.where(e_in < HALO, before, jnp.where(e_in >= SPAN - HALO, after, zone[q].astype(f32)))
            edge[q] = value.astype(bf16)

    def inside_rows(r, value):
        if r < HALO:
            return jnp.where(has_up, value, 0.0).astype(bf16)
        if r >= HALO + rows:
            return jnp.where(has_down, value, 0.0).astype(bf16)
        return value.astype(bf16)

    def unite(f, r):
        pair = conv_pair(ww_ref[...], warped[f, r - 1 : r + 3].reshape(4 * chan, cols))
        for p in range(2):
            united[r + p] = inside_rows(r + p, pair[p] + partial[r + p])

    def inner_pair(r):
        pair = conv_pair(wi_ref[...], united[r - 1 : r + 3].reshape(4 * chan, cols))
        for p in range(2):
            inner[r + p] = inside_rows(r + p, jnp.maximum(pair[p], 0.0))

    def outer_pair(r):
        pair = conv_pair(wo_ref[...], inner[r - 1 : r + 3].reshape(4 * chan, cols))
        for p in range(2):
            state[r + p - HALO] = (united[r + p].astype(f32) + pair[p]).astype(bf16)

    def inner_middle():
        for r in range(6, rows, 2):
            inner_pair(r)

    def frame(f, carry):
        arrive(row_pair(f, 0, feats))
        pack_zone(f, 0, feats, zone_f)
        for r in range(1, full - 1, 2):
            pair = conv_pair(wf_ref[...], feats[f, r - 1 : r + 3].reshape(4 * chan, cols))
            partial[r], partial[r + 1] = pair
        lay_edge(f, 0, zone_f)
        for q in range(1, qn - 1, 2):
            pair = conv_pair(wf_ref[...], edge[q - 1 : q + 3].reshape(4 * chan, LANES))
            e_part[q], e_part[q + 1] = pair

        @pl.when(f == 0)
        def _():
            for r in range(1, full - 1):
                united[r] = inside_rows(r, partial[r])
            inner_middle()

        @pl.when(f > 0)
        def _():
            spot = lax.broadcasted_iota(jnp.int32, (1, cols), 1)
            source = jnp.zeros((1, cols), jnp.int32)
            for d in range(blocks):
                source = jnp.where(spot // rows == d, slot_ref[f, 0, 0, d] * rows, source)
            index = lax.broadcasted_iota(jnp.int32, (3 * entries, cols), 0)
            placer = (index == source + spot % rows).astype(f32).astype(bf16)
            for h in range(PIECES):
                arrive(block_pair(f, h))
                part = slice(piece * h, piece * (h + 1))
                whole = jnp.concatenate([pool[f, o, part].reshape(piece * chan, entries) for o in range(3)], 1)
                placed = jnp.dot(whole, placer, preferred_element_type=f32).astype(bf16)
                warped[f, HALO + piece * h : HALO + piece * (h + 1)] = placed.reshape(piece, chan, cols)
                if h == 0:
                    start(row_pair(f, 1, warped)[:1])
            start(row_pair(f, 1, warped)[1:])
            for r in range(5, rows, 2):
                unite(f, r)
            inner_middle()
            arrive(row_pair(f, 1, warped))
            pack_zone(f, 1, warped, zone_w)
            for r in (1, 3, rows + 1, rows + 3):
                unite(f, r)

        for r in (2, 4, rows, rows + 2):
            inner_pair(r)
        for r in range(HALO, HALO + rows, 2):
            outer_pair(r)

        @pl.when(f == 0)
        def _():
            for q in range(1, qn - 1):
                e_unit[q] = jnp.where(edge_ok(q), e_part[q], 0.0).astype(bf16)

        @pl.when(f > 0)
        def _():
            lay_edge(f, 1, zone_w)
            for q in range(1, qn - 1, 2):
                pair = conv_pair(ww_ref[...], edge[q - 1 : q + 3].reshape(4 * chan, LANES))
                for p in range(2):
                    e_unit[q + p] = jnp.where(edge_ok(q + p), pair[p] + e_part[q + p], 0.0).astype(bf16)

        for q in range(2, qn - 2, 2):
            pair = conv_pair(wi_ref[...], e_unit[q - 1 : q + 3].reshape(4 * chan, LANES))
            for p in range(2):
                e_inner[q + p] = jnp.where(edge_ok(q + p), jnp.maximum(pair[p], 0.0), 0.0).astype(bf16)
        for q in range(3, qn - 3, 2):
            pair = conv_pair(wo_ref[...], e_inner[q - 1 : q + 3].reshape(4 * chan, LANES))
            for p in range(2):
                e_state[q + p - 3] = (e_unit[q + p].astype(f32) + pair[p]).astype(bf16)

        ends = e_state[...].reshape(per * chan, LANES)
        spot = lax.broadcasted_iota(jnp.int32, (per * chan, cols), 1)
        near = (spot < HALO) | (spot >= cols - HALO)
        for g in range(GROUPS):
            patch = jnp.dot(ends, patcher[g], preferred_element_type=f32)
            old = state[per * g : per * (g + 1)].reshape(per * chan, cols).astype(f32)
            state[per * g : per * (g + 1)] = jnp.where(near, patch, old).astype(bf16).reshape(per, chan, cols)

        @pl.when(f < frames - 1)
        def _():
            spot = lax.broadcasted_iota(jnp.int32, (1, entries), 1)
            index = lax.broadcasted_iota(jnp.int32, (cols, entries), 0)
            pickers = []
            for o in (0, 2, 1):
                target = jnp.zeros((1, entries), jnp.int32)
                for c in range(cap):
                    target = jnp.where(spot // rows == c, list_ref[f + 1, 0, 0, o, c] * rows, target)
                pickers.append((index == target + spot % rows).astype(f32).astype(bf16))
            both = jnp.concatenate(pickers[:2], 1)
            for h in range(PIECES):
                part = slice(piece * h, piece * (h + 1))
                whole = state[part].reshape(piece * chan, cols)
                away = jnp.dot(whole, both, preferred_element_type=f32).astype(bf16)
                offer[f + 1, 0, part] = away[:, :entries].reshape(piece, chan, entries)
                offer[f + 1, 1, part] = away[:, entries:].reshape(piece, chan, entries)
                start(block_pair(f + 1, h))
            kept = jnp.dot(state[...].reshape(rows * chan, cols), pickers[2], preferred_element_type=f32)
            pool[f + 1, 1] = kept.astype(bf16).reshape(rows, chan, entries)

        for r in range(rows):
            out_ref[f, r] = jnp.dot(wp_ref[...], state[r], preferred_element_type=f32).astype(bf16)

        sent(row_pair(f, 0, feats))
        sent(zone_pair(f, 0))

        @pl.when(f > 0)
        def _():
            sent(row_pair(f, 1, warped))
            sent(zone_pair(f, 1))
            for h in range(PIECES):
                sent(block_pair(f, h))

        return carry

    lax.fori_loop(0, frames, frame, 0)


def on_device(n_tm, n_tile, frame_feats, send_list, recv_slot, w_unite, w_inner, w_outer, w_up):
    frames, chan, rows, cols = frame_feats.shape
    planes = w_up.shape[0]
    feats = frame_feats.transpose(0, 2, 1, 3)
    entries = send_list.shape[4] * rows
    full = rows + 2 * HALO
    per = rows // GROUPS
    qn = per + 2 * HALO
    vmem = pl.BlockSpec(memory_space=pltpu.VMEM)
    smem = pl.BlockSpec(memory_space=pltpu.SMEM)

    def sems(kinds):
        return pltpu.SemaphoreType.DMA((frames, kinds, 2))

    out = pl.pallas_call(
        functools.partial(kernel, n_tm, n_tile, frames, chan, rows, cols),
        out_shape=jax.ShapeDtypeStruct((frames, rows, planes, cols), bf16),
        in_specs=[pl.BlockSpec(memory_space=pl.ANY)] + [smem] * 2 + [vmem] * 4,
        out_specs=vmem,
        scratch_shapes=[
            pltpu.VMEM((6 * chan, 4 * chan), bf16),
            pltpu.VMEM((6 * chan, 4 * chan), bf16),
            pltpu.VMEM((6 * chan, 4 * chan), bf16),
            pltpu.VMEM((6 * chan, 4 * chan), bf16),
            pltpu.VMEM((frames, full, chan, cols), bf16),
            pltpu.VMEM((frames, full, chan, cols), bf16),
            pltpu.VMEM((full, chan, cols), f32),
            pltpu.VMEM((full, chan, cols), bf16),
            pltpu.VMEM((full, chan, cols), bf16),
            pltpu.VMEM((rows, chan, cols), bf16),
            pltpu.VMEM((frames, 2, rows, chan, entries), bf16),
            pltpu.VMEM((frames, 3, rows, chan, entries), bf16),
            pltpu.VMEM((frames, 2, 2, chan, LANES), bf16),
            pltpu.VMEM((frames, 2, 2, chan, LANES), bf16),
            pltpu.VMEM((qn, chan, LANES), bf16),
            pltpu.VMEM((qn, chan, LANES), bf16),
            pltpu.VMEM((qn, chan, LANES), bf16),
            pltpu.VMEM((qn, chan, LANES), f32),
            pltpu.VMEM((qn, chan, LANES), bf16),
            pltpu.VMEM((qn, chan, LANES), bf16),
            pltpu.VMEM((per, chan, LANES), bf16),
            pltpu.VMEM((GROUPS, cols, LANES), bf16),
            pltpu.VMEM((GROUPS, LANES, cols), bf16),
            pltpu.SemaphoreType.DMA((frames,)),
            sems(2), sems(2), sems(PIECES), sems(PIECES), sems(2), sems(2),
        ],
        compiler_params=pltpu.CompilerParams(
            collective_id=0, has_side_effects=True, vmem_limit_bytes=48 * 1024 * 1024
        ),
        name="propagate",
    )(feats, send_list, recv_slot, w_unite, w_inner, w_outer, w_up)
    return out.transpose(0, 2, 1, 3)


def solution(mesh):
    placed = (
        P(None, None, "tile", "tm"),
        P(None, "tm", "tile", None, None),
        P(None, "tm", "tile", None),
        P(),
        P(),
        P(),
        P(),
    )
    return jax.shard_map(
        functools.partial(on_device, mesh.shape["tm"], mesh.shape["tile"]),
        mesh=mesh,
        in_specs=placed,
        out_specs=P(None, None, "tile", "tm"),
        check_vma=False,
    )
```

```python
import functools

import jax
import jax.numpy as jnp
from jax import lax
from jax.experimental import pallas as pl
from jax.experimental.pallas import tpu as pltpu
from jax.sharding import PartitionSpec as P

MESH = pl.DeviceIdType.MESH
HALO = 3
GROUPS = 4
SPAN = 32
LANES = GROUPS * SPAN
PIECES = 2
bf16 = jnp.bfloat16
f32 = jnp.float32


def lay_taps(taps_ref, base, matrix):
    kr, kc, out, _ = taps_ref.shape
    inp = matrix.shape[1] // kr
    for b in range(kc):
        parts = [taps_ref[a, b][:, base : base + inp].astype(f32) for a in range(kr)]
        matrix[b * out : (b + 1) * out] = jnp.concatenate(parts, 1).astype(bf16)


def conv_slab(weights, slab):
    part = jnp.dot(weights, slab, preferred_element_type=f32)
    out, n = part.shape[0] // 3, part.shape[1]
    left = pltpu.roll(part[0:out], 1, 1)
    right = pltpu.roll(part[2 * out : 3 * out], n - 1, 1)
    return left + part[out : 2 * out] + right


def kernel(
    n_tm, n_tile, frames, chan, rows, cols,
    feats_ref, list_ref, slot_ref, tu_ref, ti_ref, to_ref, wp_ref,
    out_ref,
    ww_ref, wf_ref, wi_ref, wo_ref, feats, warped, partial, united, inner, state, offer, pool,
    zone_s, zone_r, zone_f, zone_w, edge, e_part, e_unit, e_inner, e_state, packer, patcher,
    load_sem, row_send, row_recv, blk_send, blk_recv, zone_send, zone_recv,
):
    strip = lax.axis_index("tm")
    band = lax.axis_index("tile")
    has_up, has_down = band > 0, band < n_tile - 1
    has_left, has_right = strip > 0, strip < n_tm - 1
    height, width = n_tile * rows, n_tm * cols
    full = rows + 2 * HALO
    per = rows // GROUPS
    qn = per + 2 * HALO
    cap = list_ref.shape[4]
    blocks = slot_ref.shape[3]
    entries = cap * rows
    piece = rows // PIECES

    def load(f):
        return pltpu.make_async_copy(feats_ref.at[f], feats.at[f, pl.ds(HALO, rows)], load_sem.at[f])

    for f in range(frames):
        load(f).start()

    up, down = {"tile": band - 1}, {"tile": band + 1}
    left, right = {"tm": strip - 1}, {"tm": strip + 1}
    sides = ((has_up, up), (has_down, down), (has_left, left), (has_right, right))

    @pl.when(jnp.logical_not(has_up))
    def _():
        feats[:, 0:HALO] = jnp.zeros((frames, HALO, chan, cols), bf16)
        warped[:, 0:HALO] = jnp.zeros((frames, HALO, chan, cols), bf16)
        pool[:, 0] = jnp.zeros((frames, rows, chan, entries), bf16)

    @pl.when(jnp.logical_not(has_down))
    def _():
        feats[:, HALO + rows : full] = jnp.zeros((frames, HALO, chan, cols), bf16)
        warped[:, HALO + rows : full] = jnp.zeros((frames, HALO, chan, cols), bf16)
        pool[:, 2] = jnp.zeros((frames, rows, chan, entries), bf16)

    @pl.when(jnp.logical_not(has_left))
    def _():
        zone_r[:, :, 0] = jnp.zeros((frames, 2, chan, LANES), bf16)

    @pl.when(jnp.logical_not(has_right))
    def _():
        zone_r[:, :, 1] = jnp.zeros((frames, 2, chan, LANES), bf16)

    barrier = pltpu.get_barrier_semaphore()
    for there, device in sides:
        @pl.when(there)
        def _():
            pl.semaphore_signal(barrier, inc=1, device_id=device, device_id_type=MESH)

    lane = lax.broadcasted_iota(jnp.int32, (cols, LANES), 1)
    column = lax.broadcasted_iota(jnp.int32, (cols, LANES), 0)
    inside = lane % SPAN
    half = SPAN // 2
    wanted = jnp.where(
        inside < HALO,
        cols - HALO + inside,
        jnp.where(
            inside < half,
            inside - HALO,
            jnp.where(inside < SPAN - HALO, cols + HALO - SPAN + inside, inside - (SPAN - HALO)),
        ),
    )
    p_lane = lax.broadcasted_iota(jnp.int32, (LANES, cols), 0)
    p_col = lax.broadcasted_iota(jnp.int32, (LANES, cols), 1)
    p_in = p_lane % SPAN
    for g in range(GROUPS):
        packer[g] = ((lane // SPAN == g) & (column == wanted)).astype(f32).astype(bf16)
        here = jnp.where(p_in < half, p_in - HALO, cols + HALO - SPAN + p_in)
        near = (p_col < HALO) | (p_col >= cols - HALO)
        patcher[g] = ((p_lane // SPAN == g) & near & (here == p_col)).astype(f32).astype(bf16)

    for f in range(frames):
        load(f).wait()

    pl.semaphore_wait(barrier, sum(there.astype(jnp.int32) for there, _ in sides))

    def remote(src, dst, send, recv, device):
        return pltpu.make_async_remote_copy(
            src_ref=src, dst_ref=dst, send_sem=send, recv_sem=recv, device_id=device, device_id_type=MESH
        )

    def row_pair(f, kind, ref):
        return (
            (has_up, remote(ref.at[f, pl.ds(HALO, HALO)], ref.at[f, pl.ds(HALO + rows, HALO)],
                            row_send.at[f, kind, 0], row_recv.at[f, kind, 0], up), has_down),
            (has_down, remote(ref.at[f, pl.ds(rows, HALO)], ref.at[f, pl.ds(0, HALO)],
                              row_send.at[f, kind, 1], row_recv.at[f, kind, 1], down), has_up),
        )

    def block_pair(f, h):
        part = pl.ds(piece * h, piece)
        return (
            (has_down, remote(offer.at[f, 0, part], pool.at[f, 0, part],
                              blk_send.at[f, h, 0], blk_recv.at[f, h, 0], down), has_up),
            (has_up, remote(offer.at[f, 1, part], pool.at[f, 2, part],
                            blk_send.at[f, h, 1], blk_recv.at[f, h, 1], up), has_down),
        )

    def zone_pair(f, kind):
        return (
            (has_right, remote(zone_s.at[f, kind, 0], zone_r.at[f, kind, 0],
                               zone_send.at[f, kind, 0], zone_recv.at[f, kind, 0], right), has_left),
            (has_left, remote(zone_s.at[f, kind, 1], zone_r.at[f, kind, 1],
                              zone_send.at[f, kind, 1], zone_recv.at[f, kind, 1], left), has_right),
        )

    def start(pair):
        for sends, copy, _ in pair:
            pl.when(sends)(copy.start)

    def arrive(pair):
        for _, copy, gets in pair:
            pl.when(gets)(copy.wait_recv)

    def sent(pair):
        for sends, copy, _ in pair:
            pl.when(sends)(copy.wait_send)

    for f in range(frames):
        start(row_pair(f, 0, feats))
    lay_taps(tu_ref, 0, ww_ref)
    lay_taps(tu_ref, chan, wf_ref)
    lay_taps(ti_ref, 0, wi_ref)
    lay_taps(to_ref, 0, wo_ref)

    e_lane = lax.broadcasted_iota(jnp.int32, (1, LANES), 1)
    e_in = e_lane % SPAN
    e_col = strip * cols + jnp.where(e_in < half, e_in - HALO, cols + HALO - SPAN + e_in)
    col_ok = (e_col >= 0) & (e_col < width)
    e_row = band * rows + per * (e_lane // SPAN) - HALO

    def edge_ok(q):
        row = e_row + q
        return col_ok & (row >= 0) & (row < height)

    def pack_zone(f, kind, ref, zone):
        total = jnp.zeros((qn * chan, LANES), f32)
        for g in range(GROUPS):
            part = ref[f, per * g : per * g + qn].reshape(qn * chan, cols)
            total = total + jnp.dot(part, packer[g], preferred_element_type=f32)
        total = total.reshape(qn, chan, LANES)
        zone[...] = total.astype(bf16)
        last, first = total[0], pltpu.roll(total[0], LANES - (SPAN - HALO), 1)
        for q in range(1, qn):
            here = (e_in >= HALO * q) & (e_in < HALO * (q + 1))
            last = jnp.where(here, pltpu.roll(total[q], HALO * q, 1), last)
            first = jnp.where(here, pltpu.roll(total[q], (LANES - (SPAN - HALO) + HALO * q) % LANES, 1), first)
        zone_s[f, kind, 0] = last.astype(bf16)
        zone_s[f, kind, 1] = first.astype(bf16)
        start(zone_pair(f, kind))

    def lay_edge(f, kind, zone):
        arrive(zone_pair(f, kind))
        from_l, from_r = zone_r[f, kind, 0].astype(f32), zone_r[f, kind, 1].astype(f32)
        for q in range(qn):
            before = pltpu.roll(from_l, (LANES - HALO * q) % LANES, 1)
            after = pltpu.roll(from_r, (LANES + SPAN - HALO - HALO * q) % LANES, 1)
            value = jnp.where(e_in < HALO, before, jnp.where(e_in >= SPAN - HALO, after, zone[q].astype(f32)))
            edge[q] = value.astype(bf16)

    def inside_rows(r, value):
        if r < HALO:
            return jnp.where(has_up, value, 0.0).astype(bf16)
        if r >= HALO + rows:
            return jnp.where(has_down, value, 0.0).astype(bf16)
        return value.astype(bf16)

    def unite(f, r):
        value = conv_slab(ww_ref[...], warped[f, r - 1 : r + 2].reshape(3 * chan, cols))
        united[r] = inside_rows(r, value + partial[r])

    def inner_row(r):
        value = conv_slab(wi_ref[...], united[r - 1 : r + 2].reshape(3 * chan, cols))
        inner[r] = inside_rows(r, jnp.maximum(value, 0.0))

    def outer_row(r):
        value = conv_slab(wo_ref[...], inner[r - 1 : r + 2].reshape(3 * chan, cols))
        state[r - HALO] = (united[r].astype(f32) + value).astype(bf16)

    def inner_middle():
        for r in range(HALO + 2, HALO + rows - 2):
            inner_row(r)

    def frame(f, carry):
        arrive(row_pair(f, 0, feats))
        pack_zone(f, 0, feats, zone_f)
        for r in range(1, full - 1):
            partial[r] = conv_slab(wf_ref[...], feats[f, r - 1 : r + 2].reshape(3 * chan, cols))
        lay_edge(f, 0, zone_f)
        for q in range(1, qn - 1):
            e_part[q] = conv_slab(wf_ref[...], edge[q - 1 : q + 2].reshape(3 * chan, LANES))

        @pl.when(f == 0)
        def _():
            for r in range(1, full - 1):
                united[r] = inside_rows(r, partial[r])
            inner_middle()

        @pl.when(f > 0)
        def _():
            spot = lax.broadcasted_iota(jnp.int32, (1, cols), 1)
            source = jnp.zeros((1, cols), jnp.int32)
            for d in range(blocks):
                source = jnp.where(spot // rows == d, slot_ref[f, 0, 0, d] * rows, source)
            index = lax.broadcasted_iota(jnp.int32, (3 * entries, cols), 0)
            placer = (index == source + spot % rows).astype(f32).astype(bf16)
            for h in range(PIECES):
                arrive(block_pair(f, h))
                part = slice(piece * h, piece * (h + 1))
                whole = jnp.concatenate([pool[f, o, part].reshape(piece * chan, entries) for o in range(3)], 1)
                placed = jnp.dot(whole, placer, preferred_element_type=f32).astype(bf16)
                warped[f, HALO + piece * h : HALO + piece * (h + 1)] = placed.reshape(piece, chan, cols)
                if h == 0:
                    start(row_pair(f, 1, warped)[:1])
            start(row_pair(f, 1, warped)[1:])
            for r in range(HALO + 1, HALO + rows - 1):
                unite(f, r)
            inner_middle()
            arrive(row_pair(f, 1, warped))
            pack_zone(f, 1, warped, zone_w)
            for r in (1, 2, HALO, HALO + rows - 1, HALO + rows, HALO + rows + 1):
                unite(f, r)

        for r in (2, 3, 4, HALO + rows - 2, HALO + rows - 1, HALO + rows):
            inner_row(r)
        for r in range(HALO, HALO + rows):
            outer_row(r)

        @pl.when(f == 0)
        def _():
            for q in range(1, qn - 1):
                e_unit[q] = jnp.where(edge_ok(q), e_part[q], 0.0).astype(bf16)

        @pl.when(f > 0)
        def _():
            lay_edge(f, 1, zone_w)
            for q in range(1, qn - 1):
                value = conv_slab(ww_ref[...], edge[q - 1 : q + 2].reshape(3 * chan, LANES))
                e_unit[q] = jnp.where(edge_ok(q), value + e_part[q], 0.0).astype(bf16)

        for q in range(2, qn - 2):
            value = conv_slab(wi_ref[...], e_unit[q - 1 : q + 2].reshape(3 * chan, LANES))
            e_inner[q] = jnp.where(edge_ok(q), jnp.maximum(value, 0.0), 0.0).astype(bf16)
        for q in range(3, qn - 3):
            value = conv_slab(wo_ref[...], e_inner[q - 1 : q + 2].reshape(3 * chan, LANES))
            e_state[q - 3] = (e_unit[q].astype(f32) + value).astype(bf16)

        ends = e_state[...].reshape(per * chan, LANES)
        spot = lax.broadcasted_iota(jnp.int32, (per * chan, cols), 1)
        near = (spot < HALO) | (spot >= cols - HALO)
        for g in range(GROUPS):
            patch = jnp.dot(ends, patcher[g], preferred_element_type=f32)
            old = state[per * g : per * (g + 1)].reshape(per * chan, cols).astype(f32)
            state[per * g : per * (g + 1)] = jnp.where(near, patch, old).astype(bf16).reshape(per, chan, cols)

        @pl.when(f < frames - 1)
        def _():
            spot = lax.broadcasted_iota(jnp.int32, (1, entries), 1)
            index = lax.broadcasted_iota(jnp.int32, (cols, entries), 0)
            pickers = []
            for o in (0, 2, 1):
                target = jnp.zeros((1, entries), jnp.int32)
                for c in range(cap):
                    target = jnp.where(spot // rows == c, list_ref[f + 1, 0, 0, o, c] * rows, target)
                pickers.append((index == target + spot % rows).astype(f32).astype(bf16))
            both = jnp.concatenate(pickers[:2], 1)
            for h in range(PIECES):
                part = slice(piece * h, piece * (h + 1))
                whole = state[part].reshape(piece * chan, cols)
                away = jnp.dot(whole, both, preferred_element_type=f32).astype(bf16)
                offer[f + 1, 0, part] = away[:, :entries].reshape(piece, chan, entries)
                offer[f + 1, 1, part] = away[:, entries:].reshape(piece, chan, entries)
                start(block_pair(f + 1, h))
            kept = jnp.dot(state[...].reshape(rows * chan, cols), pickers[2], preferred_element_type=f32)
            pool[f + 1, 1] = kept.astype(bf16).reshape(rows, chan, entries)

        for r in range(rows):
            out_ref[f, r] = jnp.dot(wp_ref[...], state[r], preferred_element_type=f32).astype(bf16)

        sent(row_pair(f, 0, feats))
        sent(zone_pair(f, 0))

        @pl.when(f > 0)
        def _():
            sent(row_pair(f, 1, warped))
            sent(zone_pair(f, 1))
            for h in range(PIECES):
                sent(block_pair(f, h))

        return carry

    lax.fori_loop(0, frames, frame, 0)


def on_device(n_tm, n_tile, frame_feats, send_list, recv_slot, w_unite, w_inner, w_outer, w_up):
    frames, chan, rows, cols = frame_feats.shape
    planes = w_up.shape[0]
    feats = frame_feats.transpose(0, 2, 1, 3)
    entries = send_list.shape[4] * rows
    full = rows + 2 * HALO
    per = rows // GROUPS
    qn = per + 2 * HALO
    vmem = pl.BlockSpec(memory_space=pltpu.VMEM)
    smem = pl.BlockSpec(memory_space=pltpu.SMEM)

    def sems(kinds):
        return pltpu.SemaphoreType.DMA((frames, kinds, 2))

    out = pl.pallas_call(
        functools.partial(kernel, n_tm, n_tile, frames, chan, rows, cols),
        out_shape=jax.ShapeDtypeStruct((frames, rows, planes, cols), bf16),
        in_specs=[pl.BlockSpec(memory_space=pl.ANY)] + [smem] * 2 + [vmem] * 4,
        out_specs=vmem,
        scratch_shapes=[
            pltpu.VMEM((3 * chan, 3 * chan), bf16),
            pltpu.VMEM((3 * chan, 3 * chan), bf16),
            pltpu.VMEM((3 * chan, 3 * chan), bf16),
            pltpu.VMEM((3 * chan, 3 * chan), bf16),
            pltpu.VMEM((frames, full, chan, cols), bf16),
            pltpu.VMEM((frames, full, chan, cols), bf16),
            pltpu.VMEM((full, chan, cols), f32),
            pltpu.VMEM((full, chan, cols), bf16),
            pltpu.VMEM((full, chan, cols), bf16),
            pltpu.VMEM((rows, chan, cols), bf16),
            pltpu.VMEM((frames, 2, rows, chan, entries), bf16),
            pltpu.VMEM((frames, 3, rows, chan, entries), bf16),
            pltpu.VMEM((frames, 2, 2, chan, LANES), bf16),
            pltpu.VMEM((frames, 2, 2, chan, LANES), bf16),
            pltpu.VMEM((qn, chan, LANES), bf16),
            pltpu.VMEM((qn, chan, LANES), bf16),
            pltpu.VMEM((qn, chan, LANES), bf16),
            pltpu.VMEM((qn, chan, LANES), f32),
            pltpu.VMEM((qn, chan, LANES), bf16),
            pltpu.VMEM((qn, chan, LANES), bf16),
            pltpu.VMEM((per, chan, LANES), bf16),
            pltpu.VMEM((GROUPS, cols, LANES), bf16),
            pltpu.VMEM((GROUPS, LANES, cols), bf16),
            pltpu.SemaphoreType.DMA((frames,)),
            sems(2), sems(2), sems(PIECES), sems(PIECES), sems(2), sems(2),
        ],
        compiler_params=pltpu.CompilerParams(
            collective_id=0, has_side_effects=True, vmem_limit_bytes=48 * 1024 * 1024
        ),
        name="propagate",
    )(feats, send_list, recv_slot, w_unite, w_inner, w_outer, w_up)
    return out.transpose(0, 2, 1, 3)


def solution(mesh):
    placed = (
        P(None, None, "tile", "tm"),
        P(None, "tm", "tile", None, None),
        P(None, "tm", "tile", None),
        P(),
        P(),
        P(),
        P(),
    )
    return jax.shard_map(
        functools.partial(on_device, mesh.shape["tm"], mesh.shape["tile"]),
        mesh=mesh,
        in_specs=placed,
        out_specs=P(None, None, "tile", "tm"),
        check_vma=False,
    )
```

```python
import functools

import jax
import jax.numpy as jnp
from jax import lax
from jax.experimental import pallas as pl
from jax.experimental.pallas import tpu as pltpu
from jax.sharding import PartitionSpec as P

MESH = pl.DeviceIdType.MESH
HALO = 3
GROUPS = 4
SPAN = 32
LANES = GROUPS * SPAN
PIECES = 2
bf16 = jnp.bfloat16
f32 = jnp.float32


def lay_taps(taps_ref, matrix):
    kr, kc, out, inp = taps_ref.shape
    for b in range(kc):
        parts = [taps_ref[a, b].astype(f32) for a in range(kr)]
        matrix[b * out : (b + 1) * out] = jnp.concatenate(parts, 1).astype(bf16)


def conv_slab(weights, slab):
    part = jnp.dot(weights, slab, preferred_element_type=f32)
    out, n = part.shape[0] // 3, part.shape[1]
    left = pltpu.roll(part[0:out], 1, 1)
    right = pltpu.roll(part[2 * out : 3 * out], n - 1, 1)
    return left + part[out : 2 * out] + right


def kernel(
    n_tm, n_tile, frames, chan, rows, cols,
    feats_ref, list_ref, slot_ref, tu_ref, ti_ref, to_ref, wp_ref,
    out_ref,
    wu_ref, wi_ref, wo_ref, join, united, inner, state, offer, pool, zone, zone_s, zone_l, zone_r, edge, e_unit, e_inner, e_state, packer, patcher,
    load_sem, fr_send, fr_recv, wr_send, wr_recv, blk_send, blk_recv, zf_send, zf_recv, zw_send, zw_recv,
):
    strip = lax.axis_index("tm")
    band = lax.axis_index("tile")
    has_up, has_down = band > 0, band < n_tile - 1
    has_left, has_right = strip > 0, strip < n_tm - 1
    height, width = n_tile * rows, n_tm * cols
    full = rows + 2 * HALO
    qn = rows // GROUPS + 2 * HALO
    per = rows // GROUPS
    cap = list_ref.shape[4]
    blocks = slot_ref.shape[3]
    entries = cap * rows
    piece = rows // PIECES

    def load(f):
        return pltpu.make_async_copy(
            feats_ref.at[f], join.at[f, pl.ds(HALO, rows), pl.ds(chan, chan), :], load_sem.at[f]
        )

    for f in range(frames):
        load(f).start()

    up, down = {"tile": band - 1}, {"tile": band + 1}
    left, right = {"tm": strip - 1}, {"tm": strip + 1}
    sides = ((has_up, up), (has_down, down), (has_left, left), (has_right, right))

    join[0, :, 0:chan] = jnp.zeros((full, chan, cols), bf16)
    zone[0, :, 0:chan] = jnp.zeros((qn, chan, LANES), bf16)
    zone_l[0, 0:chan] = jnp.zeros((chan, LANES), bf16)
    zone_r[0, 0:chan] = jnp.zeros((chan, LANES), bf16)

    @pl.when(jnp.logical_not(has_up))
    def _():
        join[:, 0:HALO] = jnp.zeros((frames, HALO, 2 * chan, cols), bf16)
        pool[:, 0] = jnp.zeros((frames, rows, chan, entries), bf16)

    @pl.when(jnp.logical_not(has_down))
    def _():
        join[:, HALO + rows : full] = jnp.zeros((frames, HALO, 2 * chan, cols), bf16)
        pool[:, 2] = jnp.zeros((frames, rows, chan, entries), bf16)

    @pl.when(jnp.logical_not(has_left))
    def _():
        zone_l[...] = jnp.zeros(zone_l.shape, bf16)

    @pl.when(jnp.logical_not(has_right))
    def _():
        zone_r[...] = jnp.zeros(zone_r.shape, bf16)

    barrier = pltpu.get_barrier_semaphore()
    for there, device in sides:
        @pl.when(there)
        def _():
            pl.semaphore_signal(barrier, inc=1, device_id=device, device_id_type=MESH)

    lane = lax.broadcasted_iota(jnp.int32, (cols, LANES), 1)
    column = lax.broadcasted_iota(jnp.int32, (cols, LANES), 0)
    inside = lane % SPAN
    half = SPAN // 2
    wanted = jnp.where(
        inside < HALO,
        cols - HALO + inside,
        jnp.where(
            inside < half,
            inside - HALO,
            jnp.where(inside < SPAN - HALO, cols + HALO - SPAN + inside, inside - (SPAN - HALO)),
        ),
    )
    p_lane = lax.broadcasted_iota(jnp.int32, (LANES, cols), 0)
    p_col = lax.broadcasted_iota(jnp.int32, (LANES, cols), 1)
    p_in = p_lane % SPAN
    for g in range(GROUPS):
        packer[g] = ((lane // SPAN == g) & (column == wanted)).astype(f32).astype(bf16)
        here = jnp.where(p_in < half, p_in - HALO, cols + HALO - SPAN + p_in)
        near = (p_col < HALO) | (p_col >= cols - HALO)
        patcher[g] = ((p_lane // SPAN == g) & near & (here == p_col)).astype(f32).astype(bf16)

    pl.semaphore_wait(barrier, sum(there.astype(jnp.int32) for there, _ in sides))

    def remote(src, dst, send, recv, device):
        return pltpu.make_async_remote_copy(
            src_ref=src, dst_ref=dst, send_sem=send, recv_sem=recv, device_id=device, device_id_type=MESH
        )

    def row_pair(f, base, send, recv):
        part = pl.ds(base, chan)
        return (
            (has_up, remote(join.at[f, pl.ds(HALO, HALO), part, :], join.at[f, pl.ds(HALO + rows, HALO), part, :],
                            send.at[f, 0], recv.at[f, 0], up), has_down),
            (has_down, remote(join.at[f, pl.ds(rows, HALO), part, :], join.at[f, pl.ds(0, HALO), part, :],
                              send.at[f, 1], recv.at[f, 1], down), has_up),
        )

    def block_pair(f, h):
        part = pl.ds(piece * h, piece)
        return (
            (has_down, remote(offer.at[f, 0, part], pool.at[f, 0, part],
                              blk_send.at[f, h, 0], blk_recv.at[f, h, 0], down), has_up),
            (has_up, remote(offer.at[f, 1, part], pool.at[f, 2, part],
                            blk_send.at[f, h, 1], blk_recv.at[f, h, 1], up), has_down),
        )

    def zone_pair(f, base, send, recv):
        part = pl.ds(base, chan)
        return (
            (has_right, remote(zone_s.at[f, 0, part, :], zone_l.at[f, part, :],
                               send.at[f, 0], recv.at[f, 0], right), has_left),
            (has_left, remote(zone_s.at[f, 1, part, :], zone_r.at[f, part, :],
                              send.at[f, 1], recv.at[f, 1], left), has_right),
        )

    def start(pair):
        for sends, copy, _ in pair:
            pl.when(sends)(copy.start)

    def arrive(pair):
        for _, copy, gets in pair:
            pl.when(gets)(copy.wait_recv)

    def sent(pair):
        for sends, copy, _ in pair:
            pl.when(sends)(copy.wait_send)

    e_lane = lax.broadcasted_iota(jnp.int32, (1, LANES), 1)
    e_in = e_lane % SPAN

    def pack_zone(f, base):
        total = jnp.zeros((qn * chan, LANES), f32)
        for g in range(GROUPS):
            part = join[f, per * g : per * g + qn, base : base + chan, :].reshape(qn * chan, cols)
            total = total + jnp.dot(part, packer[g], preferred_element_type=f32)
        total = total.reshape(qn, chan, LANES)
        zone[f, :, base : base + chan, :] = total.astype(bf16)
        last, first = total[0], pltpu.roll(total[0], LANES - (SPAN - HALO), 1)
        for q in range(1, qn):
            here = (e_in >= HALO * q) & (e_in < HALO * (q + 1))
            last = jnp.where(here, pltpu.roll(total[q], HALO * q, 1), last)
            first = jnp.where(here, pltpu.roll(total[q], (LANES - (SPAN - HALO) + HALO * q) % LANES, 1), first)
        zone_s[f, 0, base : base + chan, :] = last.astype(bf16)
        zone_s[f, 1, base : base + chan, :] = first.astype(bf16)

    for f in range(frames):
        load(f).wait()
        start(row_pair(f, chan, fr_send, fr_recv))

    lay_taps(tu_ref, wu_ref)
    lay_taps(ti_ref, wi_ref)
    lay_taps(to_ref, wo_ref)

    e_col = strip * cols + jnp.where(e_in < half, e_in - HALO, cols + HALO - SPAN + e_in)
    col_ok = (e_col >= 0) & (e_col < width)
    e_row = band * rows + per * (e_lane // SPAN) - HALO

    def edge_ok(q):
        row = e_row + q
        return col_ok & (row >= 0) & (row < height)

    def unite_row(f, r):
        return conv_slab(wu_ref[...], join[f, pl.ds(r - 1, 3)].reshape(6 * chan, cols))

    def frame(f, carry):
        arrive(row_pair(f, chan, fr_send, fr_recv))
        pack_zone(f, chan)
        start(zone_pair(f, chan, zf_send, zf_recv))

        @pl.when(f > 0)
        def _():
            spot = lax.broadcasted_iota(jnp.int32, (1, cols), 1)
            source = jnp.zeros((1, cols), jnp.int32)
            for d in range(blocks):
                source = jnp.where(spot // rows == d, slot_ref[f, 0, 0, d] * rows, source)
            index = lax.broadcasted_iota(jnp.int32, (3 * entries, cols), 0)
            placer = (index == source + spot % rows).astype(f32).astype(bf16)
            for h in range(PIECES):
                arrive(block_pair(f, h))
                part = slice(piece * h, piece * (h + 1))
                whole = jnp.concatenate([pool[f, o, part].reshape(piece * chan, entries) for o in range(3)], 1)
                placed = jnp.dot(whole, placer, preferred_element_type=f32).astype(bf16)
                join[f, HALO + piece * h : HALO + piece * (h + 1), 0:chan, :] = placed.reshape(piece, chan, cols)
            start(row_pair(f, 0, wr_send, wr_recv))

        for r in range(HALO + 1, HALO + rows - 1):
            united[r] = unite_row(f, r).astype(bf16)

        def inner_row(r):
            slab = united[pl.ds(r - 1, 3)].reshape(3 * chan, cols)
            return jnp.maximum(conv_slab(wi_ref[...], slab), 0.0)

        for r in range(HALO + 2, HALO + rows - 2):
            inner[r] = inner_row(r).astype(bf16)

        @pl.when(f > 0)
        def _():
            arrive(row_pair(f, 0, wr_send, wr_recv))
            pack_zone(f, 0)
            start(zone_pair(f, 0, zw_send, zw_recv))

        for r in (1, 2, HALO):
            value = unite_row(f, r)
            united[r] = (value if r == HALO else jnp.where(has_up, value, 0.0)).astype(bf16)
        for r in (HALO + rows - 1, HALO + rows, HALO + rows + 1):
            value = unite_row(f, r)
            united[r] = (value if r < HALO + rows else jnp.where(has_down, value, 0.0)).astype(bf16)

        for r in (3, 4, HALO + rows - 2, HALO + rows - 1):
            inner[r] = inner_row(r).astype(bf16)
        inner[2] = jnp.where(has_up, inner_row(2), 0.0).astype(bf16)
        inner[HALO + rows] = jnp.where(has_down, inner_row(HALO + rows), 0.0).astype(bf16)

        def outer_row(r):
            slab = inner[pl.ds(r - 1, 3)].reshape(3 * chan, cols)
            state[r - HALO] = (united[r].astype(f32) + conv_slab(wo_ref[...], slab)).astype(bf16)

        for r in range(HALO, HALO + rows):
            outer_row(r)

        arrive(zone_pair(f, chan, zf_send, zf_recv))

        @pl.when(f > 0)
        def _():
            arrive(zone_pair(f, 0, zw_send, zw_recv))

        from_l, from_r = zone_l[f].astype(f32), zone_r[f].astype(f32)
        for q in range(qn):
            before = pltpu.roll(from_l, (LANES - HALO * q) % LANES, 1)
            after = pltpu.roll(from_r, (LANES + SPAN - HALO - HALO * q) % LANES, 1)
            value = jnp.where(e_in < HALO, before, jnp.where(e_in >= SPAN - HALO, after, zone[f, q].astype(f32)))
            edge[q] = value.astype(bf16)
        for q in range(1, qn - 1):
            value = conv_slab(wu_ref[...], edge[q - 1 : q + 2].reshape(6 * chan, LANES))
            e_unit[q] = jnp.where(edge_ok(q), value, 0.0).astype(bf16)
        for q in range(2, qn - 2):
            value = conv_slab(wi_ref[...], e_unit[q - 1 : q + 2].reshape(3 * chan, LANES))
            e_inner[q] = jnp.where(edge_ok(q), jnp.maximum(value, 0.0), 0.0).astype(bf16)
        for q in range(3, qn - 3):
            value = conv_slab(wo_ref[...], e_inner[q - 1 : q + 2].reshape(3 * chan, LANES))
            e_state[q - 3] = (e_unit[q].astype(f32) + value).astype(bf16)

        ends = e_state[...].reshape(per * chan, LANES)
        spot = lax.broadcasted_iota(jnp.int32, (per * chan, cols), 1)
        near = (spot < HALO) | (spot >= cols - HALO)
        for g in range(GROUPS):
            patch = jnp.dot(ends, patcher[g], preferred_element_type=f32)
            old = state[per * g : per * (g + 1)].reshape(per * chan, cols).astype(f32)
            state[per * g : per * (g + 1)] = jnp.where(near, patch, old).astype(bf16).reshape(per, chan, cols)

        @pl.when(f < frames - 1)
        def _():
            spot = lax.broadcasted_iota(jnp.int32, (1, entries), 1)
            index = lax.broadcasted_iota(jnp.int32, (cols, entries), 0)
            whole = state[...].reshape(rows * chan, cols)
            pickers = []
            for o in (0, 2, 1):
                target = jnp.zeros((1, entries), jnp.int32)
                for c in range(cap):
                    target = jnp.where(spot // rows == c, list_ref[f + 1, 0, 0, o, c] * rows, target)
                pickers.append((index == target + spot % rows).astype(f32).astype(bf16))
            both = jnp.concatenate(pickers[:2], 1)
            for h in range(PIECES):
                part = slice(piece * h, piece * (h + 1))
                away = jnp.dot(state[part].reshape(piece * chan, cols), both, preferred_element_type=f32).astype(bf16)
                offer[f + 1, 0, part] = away[:, :entries].reshape(piece, chan, entries)
                offer[f + 1, 1, part] = away[:, entries:].reshape(piece, chan, entries)
                start(block_pair(f + 1, h))
            kept = jnp.dot(whole, pickers[2], preferred_element_type=f32).astype(bf16)
            pool[f + 1, 1] = kept.reshape(rows, chan, entries)

        for r in range(rows):
            out_ref[f, r] = jnp.dot(wp_ref[...], state[r], preferred_element_type=f32).astype(bf16)

        sent(row_pair(f, chan, fr_send, fr_recv))
        sent(zone_pair(f, chan, zf_send, zf_recv))

        @pl.when(f > 0)
        def _():
            sent(row_pair(f, 0, wr_send, wr_recv))
            sent(zone_pair(f, 0, zw_send, zw_recv))
            for h in range(PIECES):
                sent(block_pair(f, h))

        return carry

    lax.fori_loop(0, frames, frame, 0)


def on_device(n_tm, n_tile, frame_feats, send_list, recv_slot, w_unite, w_inner, w_outer, w_up):
    frames, chan, rows, cols = frame_feats.shape
    planes = w_up.shape[0]
    feats = frame_feats.transpose(0, 2, 1, 3)
    entries = send_list.shape[4] * rows
    full = rows + 2 * HALO
    per = rows // GROUPS
    qn = per + 2 * HALO
    vmem = pl.BlockSpec(memory_space=pltpu.VMEM)
    smem = pl.BlockSpec(memory_space=pltpu.SMEM)
    sems = pltpu.SemaphoreType.DMA((frames, 2))
    out = pl.pallas_call(
        functools.partial(kernel, n_tm, n_tile, frames, chan, rows, cols),
        out_shape=jax.ShapeDtypeStruct((frames, rows, planes, cols), bf16),
        in_specs=[pl.BlockSpec(memory_space=pl.ANY)] + [smem] * 2 + [vmem] * 4,
        out_specs=vmem,
        scratch_shapes=[
            pltpu.VMEM((3 * chan, 6 * chan), bf16),
            pltpu.VMEM((3 * chan, 3 * chan), bf16),
            pltpu.VMEM((3 * chan, 3 * chan), bf16),
            pltpu.VMEM((frames, full, 2 * chan, cols), bf16),
            pltpu.VMEM((full, chan, cols), bf16),
            pltpu.VMEM((full, chan, cols), bf16),
            pltpu.VMEM((rows, chan, cols), bf16),
            pltpu.VMEM((frames, 2, rows, chan, entries), bf16),
            pltpu.VMEM((frames, 3, rows, chan, entries), bf16),
            pltpu.VMEM((frames, qn, 2 * chan, LANES), bf16),
            pltpu.VMEM((frames, 2, 2 * chan, LANES), bf16),
            pltpu.VMEM((frames, 2 * chan, LANES), bf16),
            pltpu.VMEM((frames, 2 * chan, LANES), bf16),
            pltpu.VMEM((qn, 2 * chan, LANES), bf16),
            pltpu.VMEM((qn, chan, LANES), bf16),
            pltpu.VMEM((qn, chan, LANES), bf16),
            pltpu.VMEM((per, chan, LANES), bf16),
            pltpu.VMEM((GROUPS, cols, LANES), bf16),
            pltpu.VMEM((GROUPS, LANES, cols), bf16),
            pltpu.SemaphoreType.DMA((frames,)),
        ] + [sems] * 4 + [pltpu.SemaphoreType.DMA((frames, PIECES, 2))] * 2 + [sems] * 4,
        compiler_params=pltpu.CompilerParams(
            collective_id=0, has_side_effects=True, vmem_limit_bytes=48 * 1024 * 1024
        ),
        name="propagate",
    )(feats, send_list, recv_slot, w_unite, w_inner, w_outer, w_up)
    return out.transpose(0, 2, 1, 3)


def solution(mesh):
    placed = (
        P(None, None, "tile", "tm"),
        P(None, "tm", "tile", None, None),
        P(None, "tm", "tile", None),
        P(),
        P(),
        P(),
        P(),
    )
    return jax.shard_map(
        functools.partial(on_device, mesh.shape["tm"], mesh.shape["tile"]),
        mesh=mesh,
        in_specs=placed,
        out_specs=P(None, None, "tile", "tm"),
        check_vma=False,
    )
```

```python
import functools

import jax
import jax.numpy as jnp
from jax import lax
from jax.experimental import pallas as pl
from jax.experimental.pallas import tpu as pltpu
from jax.sharding import PartitionSpec as P

MESH = pl.DeviceIdType.MESH
HALO = 3
GROUPS = 4
SPAN = 32
LANES = GROUPS * SPAN
PIECES = 2
bf16 = jnp.bfloat16
f32 = jnp.float32


def lay_taps(taps_ref, matrix):
    kr, kc, out, inp = taps_ref.shape
    for b in range(kc):
        parts = [taps_ref[a, b].astype(f32) for a in range(kr)]
        matrix[b * out : (b + 1) * out] = jnp.concatenate(parts, 1).astype(bf16)


def conv_slab(weights, slab):
    part = jnp.dot(weights, slab, preferred_element_type=f32)
    out, n = part.shape[0] // 3, part.shape[1]
    left = pltpu.roll(part[0:out], 1, 1)
    right = pltpu.roll(part[2 * out : 3 * out], n - 1, 1)
    return left + part[out : 2 * out] + right


def looped(first, count, step, body):
    def go(i, carry):
        for k in range(step):
            body(first + i * step + k)
        return carry

    lax.fori_loop(0, count // step, go, 0)


def kernel(
    n_tm, n_tile, frames, chan, rows, cols,
    feats_ref, list_ref, slot_ref, tu_ref, ti_ref, to_ref, wp_ref,
    out_ref,
    wu_ref, wi_ref, wo_ref, join, united, inner, state, offer, pool, zone, zone_s, zone_l, zone_r, edge, e_unit, e_inner, e_state, packer, patcher,
    load_sem, fr_send, fr_recv, wr_send, wr_recv, blk_send, blk_recv, zf_send, zf_recv, zw_send, zw_recv,
):
    strip = lax.axis_index("tm")
    band = lax.axis_index("tile")
    has_up, has_down = band > 0, band < n_tile - 1
    has_left, has_right = strip > 0, strip < n_tm - 1
    height, width = n_tile * rows, n_tm * cols
    full = rows + 2 * HALO
    qn = rows // GROUPS + 2 * HALO
    per = rows // GROUPS
    cap = list_ref.shape[4]
    blocks = slot_ref.shape[3]
    entries = cap * rows
    piece = rows // PIECES

    def load(f):
        return pltpu.make_async_copy(
            feats_ref.at[f], join.at[f, pl.ds(HALO, rows), pl.ds(chan, chan), :], load_sem.at[f]
        )

    for f in range(frames):
        load(f).start()

    up, down = {"tile": band - 1}, {"tile": band + 1}
    left, right = {"tm": strip - 1}, {"tm": strip + 1}
    sides = ((has_up, up), (has_down, down), (has_left, left), (has_right, right))

    join[0, :, 0:chan] = jnp.zeros((full, chan, cols), bf16)
    zone[0, :, 0:chan] = jnp.zeros((qn, chan, LANES), bf16)
    zone_l[0, 0:chan] = jnp.zeros((chan, LANES), bf16)
    zone_r[0, 0:chan] = jnp.zeros((chan, LANES), bf16)

    @pl.when(jnp.logical_not(has_up))
    def _():
        join[:, 0:HALO] = jnp.zeros((frames, HALO, 2 * chan, cols), bf16)
        pool[:, 0] = jnp.zeros((frames, rows, chan, entries), bf16)

    @pl.when(jnp.logical_not(has_down))
    def _():
        join[:, HALO + rows : full] = jnp.zeros((frames, HALO, 2 * chan, cols), bf16)
        pool[:, 2] = jnp.zeros((frames, rows, chan, entries), bf16)

    @pl.when(jnp.logical_not(has_left))
    def _():
        zone_l[...] = jnp.zeros(zone_l.shape, bf16)

    @pl.when(jnp.logical_not(has_right))
    def _():
        zone_r[...] = jnp.zeros(zone_r.shape, bf16)

    barrier = pltpu.get_barrier_semaphore()
    for there, device in sides:
        @pl.when(there)
        def _():
            pl.semaphore_signal(barrier, inc=1, device_id=device, device_id_type=MESH)

    lane = lax.broadcasted_iota(jnp.int32, (cols, LANES), 1)
    column = lax.broadcasted_iota(jnp.int32, (cols, LANES), 0)
    inside = lane % SPAN
    half = SPAN // 2
    wanted = jnp.where(
        inside < HALO,
        cols - HALO + inside,
        jnp.where(
            inside < half,
            inside - HALO,
            jnp.where(inside < SPAN - HALO, cols + HALO - SPAN + inside, inside - (SPAN - HALO)),
        ),
    )
    p_lane = lax.broadcasted_iota(jnp.int32, (LANES, cols), 0)
    p_col = lax.broadcasted_iota(jnp.int32, (LANES, cols), 1)
    p_in = p_lane % SPAN
    for g in range(GROUPS):
        packer[g] = ((lane // SPAN == g) & (column == wanted)).astype(f32).astype(bf16)
        here = jnp.where(p_in < half, p_in - HALO, cols + HALO - SPAN + p_in)
        near = (p_col < HALO) | (p_col >= cols - HALO)
        patcher[g] = ((p_lane // SPAN == g) & near & (here == p_col)).astype(f32).astype(bf16)

    pl.semaphore_wait(barrier, sum(there.astype(jnp.int32) for there, _ in sides))

    def remote(src, dst, send, recv, device):
        return pltpu.make_async_remote_copy(
            src_ref=src, dst_ref=dst, send_sem=send, recv_sem=recv, device_id=device, device_id_type=MESH
        )

    def row_pair(f, base, send, recv):
        part = pl.ds(base, chan)
        return (
            (has_up, remote(join.at[f, pl.ds(HALO, HALO), part, :], join.at[f, pl.ds(HALO + rows, HALO), part, :],
                            send.at[f, 0], recv.at[f, 0], up), has_down),
            (has_down, remote(join.at[f, pl.ds(rows, HALO), part, :], join.at[f, pl.ds(0, HALO), part, :],
                              send.at[f, 1], recv.at[f, 1], down), has_up),
        )

    def block_pair(f, h):
        part = pl.ds(piece * h, piece)
        return (
            (has_down, remote(offer.at[f, 0, part], pool.at[f, 0, part],
                              blk_send.at[f, h, 0], blk_recv.at[f, h, 0], down), has_up),
            (has_up, remote(offer.at[f, 1, part], pool.at[f, 2, part],
                            blk_send.at[f, h, 1], blk_recv.at[f, h, 1], up), has_down),
        )

    def zone_pair(f, base, send, recv):
        part = pl.ds(base, chan)
        return (
            (has_right, remote(zone_s.at[f, 0, part, :], zone_l.at[f, part, :],
                               send.at[f, 0], recv.at[f, 0], right), has_left),
            (has_left, remote(zone_s.at[f, 1, part, :], zone_r.at[f, part, :],
                              send.at[f, 1], recv.at[f, 1], left), has_right),
        )

    def start(pair):
        for sends, copy, _ in pair:
            pl.when(sends)(copy.start)

    def arrive(pair):
        for _, copy, gets in pair:
            pl.when(gets)(copy.wait_recv)

    def sent(pair):
        for sends, copy, _ in pair:
            pl.when(sends)(copy.wait_send)

    e_lane = lax.broadcasted_iota(jnp.int32, (1, LANES), 1)
    e_in = e_lane % SPAN

    def pack_zone(f, base):
        total = jnp.zeros((qn * chan, LANES), f32)
        for g in range(GROUPS):
            part = join[f, per * g : per * g + qn, base : base + chan, :].reshape(qn * chan, cols)
            total = total + jnp.dot(part, packer[g], preferred_element_type=f32)
        total = total.reshape(qn, chan, LANES)
        zone[f, :, base : base + chan, :] = total.astype(bf16)
        last, first = total[0], pltpu.roll(total[0], LANES - (SPAN - HALO), 1)
        for q in range(1, qn):
            here = (e_in >= HALO * q) & (e_in < HALO * (q + 1))
            last = jnp.where(here, pltpu.roll(total[q], HALO * q, 1), last)
            first = jnp.where(here, pltpu.roll(total[q], (LANES - (SPAN - HALO) + HALO * q) % LANES, 1), first)
        zone_s[f, 0, base : base + chan, :] = last.astype(bf16)
        zone_s[f, 1, base : base + chan, :] = first.astype(bf16)

    for f in range(frames):
        load(f).wait()
        start(row_pair(f, chan, fr_send, fr_recv))

    lay_taps(tu_ref, wu_ref)
    lay_taps(ti_ref, wi_ref)
    lay_taps(to_ref, wo_ref)

    e_col = strip * cols + jnp.where(e_in < half, e_in - HALO, cols + HALO - SPAN + e_in)
    col_ok = (e_col >= 0) & (e_col < width)
    e_row = band * rows + per * (e_lane // SPAN) - HALO

    def edge_ok(q):
        row = e_row + q
        return col_ok & (row >= 0) & (row < height)

    def unite_row(f, r):
        return conv_slab(wu_ref[...], join[f, pl.ds(r - 1, 3)].reshape(6 * chan, cols))

    def frame(f, carry):
        arrive(row_pair(f, chan, fr_send, fr_recv))
        pack_zone(f, chan)
        start(zone_pair(f, chan, zf_send, zf_recv))

        @pl.when(f > 0)
        def _():
            spot = lax.broadcasted_iota(jnp.int32, (1, cols), 1)
            source = jnp.zeros((1, cols), jnp.int32)
            for d in range(blocks):
                source = jnp.where(spot // rows == d, slot_ref[f, 0, 0, d] * rows, source)
            index = lax.broadcasted_iota(jnp.int32, (3 * entries, cols), 0)
            placer = (index == source + spot % rows).astype(f32).astype(bf16)
            for h in range(PIECES):
                arrive(block_pair(f, h))
                part = slice(piece * h, piece * (h + 1))
                whole = jnp.concatenate([pool[f, o, part].reshape(piece * chan, entries) for o in range(3)], 1)
                placed = jnp.dot(whole, placer, preferred_element_type=f32).astype(bf16)
                join[f, HALO + piece * h : HALO + piece * (h + 1), 0:chan, :] = placed.reshape(piece, chan, cols)
            start(row_pair(f, 0, wr_send, wr_recv))

        def unite_inside(r):
            united[r] = unite_row(f, r).astype(bf16)

        looped(HALO + 1, rows - 2, 7, unite_inside)

        def inner_row(r):
            slab = united[pl.ds(r - 1, 3)].reshape(3 * chan, cols)
            return jnp.maximum(conv_slab(wi_ref[...], slab), 0.0)

        def inner_inside(r):
            inner[r] = inner_row(r).astype(bf16)

        looped(HALO + 2, rows - 4, 6, inner_inside)

        @pl.when(f > 0)
        def _():
            arrive(row_pair(f, 0, wr_send, wr_recv))
            pack_zone(f, 0)
            start(zone_pair(f, 0, zw_send, zw_recv))

        for r in (1, 2, HALO):
            value = unite_row(f, r)
            united[r] = (value if r == HALO else jnp.where(has_up, value, 0.0)).astype(bf16)
        for r in (HALO + rows - 1, HALO + rows, HALO + rows + 1):
            value = unite_row(f, r)
            united[r] = (value if r < HALO + rows else jnp.where(has_down, value, 0.0)).astype(bf16)

        for r in (3, 4, HALO + rows - 2, HALO + rows - 1):
            inner[r] = inner_row(r).astype(bf16)
        inner[2] = jnp.where(has_up, inner_row(2), 0.0).astype(bf16)
        inner[HALO + rows] = jnp.where(has_down, inner_row(HALO + rows), 0.0).astype(bf16)

        def outer_row(r):
            slab = inner[pl.ds(r - 1, 3)].reshape(3 * chan, cols)
            state[r - HALO] = (united[r].astype(f32) + conv_slab(wo_ref[...], slab)).astype(bf16)

        looped(HALO, rows, 8, outer_row)

        arrive(zone_pair(f, chan, zf_send, zf_recv))

        @pl.when(f > 0)
        def _():
            arrive(zone_pair(f, 0, zw_send, zw_recv))

        from_l, from_r = zone_l[f].astype(f32), zone_r[f].astype(f32)
        for q in range(qn):
            before = pltpu.roll(from_l, (LANES - HALO * q) % LANES, 1)
            after = pltpu.roll(from_r, (LANES + SPAN - HALO - HALO * q) % LANES, 1)
            value = jnp.where(e_in < HALO, before, jnp.where(e_in >= SPAN - HALO, after, zone[f, q].astype(f32)))
            edge[q] = value.astype(bf16)
        for q in range(1, qn - 1):
            value = conv_slab(wu_ref[...], edge[q - 1 : q + 2].reshape(6 * chan, LANES))
            e_unit[q] = jnp.where(edge_ok(q), value, 0.0).astype(bf16)
        for q in range(2, qn - 2):
            value = conv_slab(wi_ref[...], e_unit[q - 1 : q + 2].reshape(3 * chan, LANES))
            e_inner[q] = jnp.where(edge_ok(q), jnp.maximum(value, 0.0), 0.0).astype(bf16)
        for q in range(3, qn - 3):
            value = conv_slab(wo_ref[...], e_inner[q - 1 : q + 2].reshape(3 * chan, LANES))
            e_state[q - 3] = (e_unit[q].astype(f32) + value).astype(bf16)

        ends = e_state[...].reshape(per * chan, LANES)
        spot = lax.broadcasted_iota(jnp.int32, (per * chan, cols), 1)
        near = (spot < HALO) | (spot >= cols - HALO)
        for g in range(GROUPS):
            patch = jnp.dot(ends, patcher[g], preferred_element_type=f32)
            old = state[per * g : per * (g + 1)].reshape(per * chan, cols).astype(f32)
            state[per * g : per * (g + 1)] = jnp.where(near, patch, old).astype(bf16).reshape(per, chan, cols)

        @pl.when(f < frames - 1)
        def _():
            spot = lax.broadcasted_iota(jnp.int32, (1, entries), 1)
            index = lax.broadcasted_iota(jnp.int32, (cols, entries), 0)
            whole = state[...].reshape(rows * chan, cols)
            pickers = []
            for o in (0, 2, 1):
                target = jnp.zeros((1, entries), jnp.int32)
                for c in range(cap):
                    target = jnp.where(spot // rows == c, list_ref[f + 1, 0, 0, o, c] * rows, target)
                pickers.append((index == target + spot % rows).astype(f32).astype(bf16))
            both = jnp.concatenate(pickers[:2], 1)
            for h in range(PIECES):
                part = slice(piece * h, piece * (h + 1))
                away = jnp.dot(state[part].reshape(piece * chan, cols), both, preferred_element_type=f32).astype(bf16)
                offer[f + 1, 0, part] = away[:, :entries].reshape(piece, chan, entries)
                offer[f + 1, 1, part] = away[:, entries:].reshape(piece, chan, entries)
                start(block_pair(f + 1, h))
            kept = jnp.dot(whole, pickers[2], preferred_element_type=f32).astype(bf16)
            pool[f + 1, 1] = kept.reshape(rows, chan, entries)

        for r in range(rows):
            out_ref[f, r] = jnp.dot(wp_ref[...], state[r], preferred_element_type=f32).astype(bf16)

        sent(row_pair(f, chan, fr_send, fr_recv))
        sent(zone_pair(f, chan, zf_send, zf_recv))

        @pl.when(f > 0)
        def _():
            sent(row_pair(f, 0, wr_send, wr_recv))
            sent(zone_pair(f, 0, zw_send, zw_recv))
            for h in range(PIECES):
                sent(block_pair(f, h))

        return carry

    lax.fori_loop(0, frames, frame, 0)


def on_device(n_tm, n_tile, frame_feats, send_list, recv_slot, w_unite, w_inner, w_outer, w_up):
    frames, chan, rows, cols = frame_feats.shape
    planes = w_up.shape[0]
    feats = frame_feats.transpose(0, 2, 1, 3)
    entries = send_list.shape[4] * rows
    full = rows + 2 * HALO
    per = rows // GROUPS
    qn = per + 2 * HALO
    vmem = pl.BlockSpec(memory_space=pltpu.VMEM)
    smem = pl.BlockSpec(memory_space=pltpu.SMEM)
    sems = pltpu.SemaphoreType.DMA((frames, 2))
    out = pl.pallas_call(
        functools.partial(kernel, n_tm, n_tile, frames, chan, rows, cols),
        out_shape=jax.ShapeDtypeStruct((frames, rows, planes, cols), bf16),
        in_specs=[pl.BlockSpec(memory_space=pl.ANY)] + [smem] * 2 + [vmem] * 4,
        out_specs=vmem,
        scratch_shapes=[
            pltpu.VMEM((3 * chan, 6 * chan), bf16),
            pltpu.VMEM((3 * chan, 3 * chan), bf16),
            pltpu.VMEM((3 * chan, 3 * chan), bf16),
            pltpu.VMEM((frames, full, 2 * chan, cols), bf16),
            pltpu.VMEM((full, chan, cols), bf16),
            pltpu.VMEM((full, chan, cols), bf16),
            pltpu.VMEM((rows, chan, cols), bf16),
            pltpu.VMEM((frames, 2, rows, chan, entries), bf16),
            pltpu.VMEM((frames, 3, rows, chan, entries), bf16),
            pltpu.VMEM((frames, qn, 2 * chan, LANES), bf16),
            pltpu.VMEM((frames, 2, 2 * chan, LANES), bf16),
            pltpu.VMEM((frames, 2 * chan, LANES), bf16),
            pltpu.VMEM((frames, 2 * chan, LANES), bf16),
            pltpu.VMEM((qn, 2 * chan, LANES), bf16),
            pltpu.VMEM((qn, chan, LANES), bf16),
            pltpu.VMEM((qn, chan, LANES), bf16),
            pltpu.VMEM((per, chan, LANES), bf16),
            pltpu.VMEM((GROUPS, cols, LANES), bf16),
            pltpu.VMEM((GROUPS, LANES, cols), bf16),
            pltpu.SemaphoreType.DMA((frames,)),
        ] + [sems] * 4 + [pltpu.SemaphoreType.DMA((frames, PIECES, 2))] * 2 + [sems] * 4,
        compiler_params=pltpu.CompilerParams(
            collective_id=0, has_side_effects=True, vmem_limit_bytes=48 * 1024 * 1024
        ),
        name="propagate",
    )(feats, send_list, recv_slot, w_unite, w_inner, w_outer, w_up)
    return out.transpose(0, 2, 1, 3)


def solution(mesh):
    placed = (
        P(None, None, "tile", "tm"),
        P(None, "tm", "tile", None, None),
        P(None, "tm", "tile", None),
        P(),
        P(),
        P(),
        P(),
    )
    return jax.shard_map(
        functools.partial(on_device, mesh.shape["tm"], mesh.shape["tile"]),
        mesh=mesh,
        in_specs=placed,
        out_specs=P(None, None, "tile", "tm"),
        check_vma=False,
    )
```
